128 devices in a mesh: proto: 16 (over x, z), design: 8 (over y, core).
Axes of the slice: x: 4, y: 4, z: 4, core: 2. Of those that a mesh axis runs over, the one named last changes fastest.
Arguments:
- designs: bfloat16 [131072, 1024], P(('proto', 'design')), may hold values from -32 to 32
- prototypes: float32 [32768, 1024], P('proto'), may hold values from -6 to 6
- candidates: int32 [128, 24], P(('proto', 'design')), may hold values from 0 to 255, as said below
- positives: int32 [131072], P(('proto', 'design')), may hold values from 0 to 32767, as said below
Outputs:
- losses: float32 [131072], P(('proto', 'design'))
- design_grad: bfloat16 [131072, 1024], P(('proto', 'design'))
- proto_grad: float32 [32768, 1024], P(('proto', 'design'))
The draws below stay inside these ranges and needn't reach their ends.
Inputs may be any that keep to these rules, and one draw needn't show every extreme that they name: `candidates`: row g lists 24 distinct blocks for the designs of device g along proto+design. Block b lies in proto shard b // 16; at most 2 blocks of a row lie in one proto shard, and in every draw one shard holds exactly 2 blocks of every row. `positives`: the positive row of design i lies in one of the blocks of row i // 1024 of candidates.
All inputs are finite; a program needn't handle non-finite values.
Results may differ from the reference program's by a relative error of at most 0.0062.
Values may be sent and summed in bfloat16 or wider, within the bound.
A program may use at most 128 MiB of HBM per device.

```python
import jax
import jax.numpy as jnp
from jax import lax

D = 1024
TILE = 128
B_DEV = 1024
BLOCKS_DEV = 16
CANDS = 24
DESIGNS = 131072
PROTOS = 32768
N_PROTO = 16
N_DESIGN = 8


def candidate_table(key):
    dev_count = N_PROTO * N_DESIGN
    capacity = max(2, (4 * CANDS + 3 * N_PROTO - 1) // (3 * N_PROTO))
    least_full = max(1, -((N_PROTO - CANDS) // (capacity - 1)))
    most_full = CANDS // capacity
    key_pop, key_hot, key_jitter, key_full, key_block, key_shuffle = jax.random.split(key, 6)
    owner_ids = jnp.arange(N_PROTO, dtype=jnp.int32)
    popular = jax.random.randint(key_pop, (N_PROTO,), 0, 4)
    hot_owner = jax.random.randint(key_hot, (), 0, N_PROTO)
    popular = jnp.where(owner_ids == hot_owner, 8, popular)
    jitter = jax.random.randint(key_jitter, (dev_count, N_PROTO), 0, N_PROTO)
    scores = (popular[None, :] * N_PROTO + jitter) * N_PROTO + owner_ids[None, :]
    ranking = jnp.argsort(-scores, axis=1).astype(jnp.int32)
    full_count = jax.random.randint(key_full, (dev_count, 1), least_full, most_full + 1)
    entries = jnp.arange(CANDS, dtype=jnp.int32)[None, :]
    full_slots = full_count * capacity
    rank_of = jnp.where(entries < full_slots, entries // capacity, full_count + entries - full_slots)
    copy_index = jnp.where(entries < full_slots, entries % capacity, 0)
    owners = jnp.take_along_axis(ranking, rank_of, axis=1)
    block_scores = jax.random.randint(key_block, (dev_count, N_PROTO, BLOCKS_DEV), 0, 2 ** 20) * BLOCKS_DEV + jnp.arange(BLOCKS_DEV, dtype=jnp.int32)
    block_order = jnp.argsort(block_scores, axis=2).astype(jnp.int32)
    device_ids = jnp.arange(dev_count, dtype=jnp.int32)[:, None]
    local_ids = block_order[device_ids, owners, copy_index]
    block_ids = owners * BLOCKS_DEV + local_ids
    shuffle = jnp.argsort(jax.random.randint(key_shuffle, (dev_count, CANDS), 0, 2 ** 20) * CANDS + entries, axis=1)
    return jnp.take_along_axis(block_ids, shuffle, axis=1).astype(jnp.int32)


def prototype_values(key):
    key_main = jax.random.fold_in(jax.random.fold_in(key, 21), 0)
    values = jax.random.normal(key_main, (PROTOS, D), jnp.float32)
    return jnp.clip(values, -6.0, 6.0)


def draw_candidates(key, part):
    return candidate_table(jax.random.fold_in(key, 11))


def draw_positives(key, part):
    dev_count = N_PROTO * N_DESIGN
    block_table = candidate_table(jax.random.fold_in(key, 11))
    chosen = jax.random.randint(jax.random.fold_in(key, 12), (dev_count, B_DEV), 0, CANDS)
    within = jax.random.randint(jax.random.fold_in(key, 13), (dev_count, B_DEV), 0, TILE)
    blocks = jnp.take_along_axis(block_table, chosen, axis=1)
    return (blocks * TILE + within).reshape(-1).astype(jnp.int32)


def draw_prototypes(key, part):
    return prototype_values(key)


def draw_designs(key, part):
    key_main = jax.random.fold_in(jax.random.fold_in(key, 31), 0)
    values = jax.random.normal(key_main, (DESIGNS, D), jnp.float32)
    return jnp.clip(values, -32.0, 32.0).astype(jnp.bfloat16)


def setup_inputs(seed: int = 0) -> dict:
    splits = jax.random.split(jax.random.key(seed), 5)
    return {
        "designs": draw_designs(jax.random.fold_in(splits[4], 71), 0),
        "prototypes": draw_prototypes(jax.random.fold_in(splits[4], 71), 0),
        "candidates": draw_candidates(jax.random.fold_in(splits[4], 71), 0),
        "positives": draw_positives(jax.random.fold_in(splits[4], 71), 0),
    }


def contrast(design_rows, cand_rows, block_list, positive_ids):
    logit_scale = D ** -0.5
    logits = lax.dot_general(design_rows, cand_rows, (((1,), (1,)), ((), ())), preferred_element_type=jnp.float32) * logit_scale
    cand_count = block_list.shape[0]
    block_match = (positive_ids // TILE)[:, None] == block_list[None, :]
    cand_index = jnp.sum(jnp.where(block_match, jnp.arange(cand_count, dtype=jnp.int32)[None, :], 0), axis=1)
    positive_col = cand_index * TILE + positive_ids % TILE
    columns = jnp.arange(cand_count * TILE, dtype=jnp.int32)
    target = columns[None, :] == positive_col[:, None]
    row_max = jnp.max(logits, axis=1, keepdims=True)
    log_total = row_max + jnp.log(jnp.sum(jnp.exp(logits - row_max), axis=1, keepdims=True))
    picked = jnp.sum(jnp.where(target, logits, 0.0), axis=1)
    losses = log_total[:, 0] - picked
    chances = jnp.exp(logits - log_total)
    logit_grad = (chances - target.astype(jnp.float32)).astype(jnp.bfloat16)
    design_grad = jnp.dot(logit_grad, cand_rows, preferred_element_type=jnp.float32).astype(jnp.bfloat16)
    return losses, design_grad, logit_grad


def reference(designs, prototypes, candidates, positives):
    dev_count = N_PROTO * N_DESIGN
    block_count = PROTOS // TILE
    feature_width = designs.shape[1]
    proto_table = prototypes.astype(jnp.bfloat16).reshape(block_count, TILE, feature_width)

    def visit_device(summed, inputs):
        design_rows, block_list, positive_ids = inputs
        cand_rows = jnp.take(proto_table, block_list, axis=0).reshape(-1, feature_width)
        losses, design_grad, logit_grad = contrast(design_rows, cand_rows, block_list, positive_ids)
        tile_grad = lax.dot_general(logit_grad, design_rows, (((0,), (0,)), ((), ())), preferred_element_type=jnp.float32)
        summed = summed.at[block_list].add(tile_grad.reshape(-1, TILE, feature_width))
        return summed, (losses, design_grad)

    initial = jnp.zeros((block_count, TILE, feature_width), jnp.float32)
    summed, outputs = lax.scan(visit_device, initial, (designs.reshape(dev_count, B_DEV, feature_width), candidates, positives.reshape(dev_count, B_DEV)))
    losses, design_grad = outputs
    return losses.reshape(-1), design_grad.reshape(-1, feature_width), summed.reshape(-1, feature_width)
```

```python
import jax
import jax.numpy as jnp
from jax import lax
from jax.experimental import pallas as pl
from jax.experimental.pallas import tpu as pltpu
from jax.sharding import PartitionSpec as P

D = 1024
HALF = 512
TILE = 128
ROWS = 1024
SIDE = 4
BLOCKS = 16
CANDS = 24
PAIR = 2 * TILE
COLS = 256
LOW = -3.0e38
MESH = pl.DeviceIdType.MESH
BF16 = jnp.bfloat16
F32 = jnp.float32
I32 = jnp.int32


def remote(src, dst, send_sem, recv_sem, device):
    return pltpu.make_async_remote_copy(
        src_ref=src, dst_ref=dst, send_sem=send_sem, recv_sem=recv_sem, device_id=device, device_id_type=MESH
    )


def iota(shape, dim):
    return lax.broadcasted_iota(I32, shape, dim)


def to_column(row):
    n = row.shape[1]
    return jnp.sum(jnp.where(iota((n, n), 0) == iota((n, n), 1), jnp.broadcast_to(row, (n, n)), 0), axis=1, keepdims=True)


def to_row(col):
    n = col.shape[0]
    return jnp.sum(jnp.where(iota((n, n), 0) == iota((n, n), 1), jnp.broadcast_to(col, (n, n)), 0), axis=0, keepdims=True)


def gray(k):
    return k + (k // 2) * (1 - 2 * (k % 2))


def pair_of(n):
    s = jnp.where(n >= 1, 1, 0) + jnp.where(n >= 4, 1, 0) + jnp.where(n >= 9, 1, 0)
    m = n - s * s
    return gray(jnp.minimum(s, 2 * s - m)), gray(jnp.minimum(m, s))


def kernel(
    des, proto, cand, pos, loss_o, dg_o, pg_o,
    tab0, tab1, tab2, tab3, rr0, rr1, rr2, rr3,
    send, arr_m, arr_o, des_m, des_o, dt_m, dt_o, grads, stage, merge, from_up, from_down, from_y, runs, core_in, dg_s,
    prow, m_run, s_run, pick, total, req_v, req_in, order_v, req_own, req_s, order_s,
    ld_sem, des_sem, out_sem, loc_sem, own_sem, rq_s, rq_r, ag_s, ag_r, rl_s, rl_r, f_s, fm_r, fo_r, b_s, b_r,
    mg_s, mg_r, rs_s, rs_r, y_s, y_r, c_s, c_r,
):
    p, d = lax.axis_index("proto"), lax.axis_index("design")
    x, z, y, r = p // SIDE, p % SIDE, d // 2, d % 2
    tab, rr = (tab0, tab1, tab2, tab3), (rr0, rr1, rr2, rr3)

    def owner(ku, kv):
        return ((x + ku * (1 - r) + kv * r) % SIDE) * SIDE + (z + ku * r + kv * (1 - r)) % SIDE

    def along_u(k, core):
        return (owner(k, 0), y * 2 + core)

    def along_v(k, core):
        return (owner(0, k), y * 2 + core)

    sibling = (p, y * 2 + 1 - r)
    my_cols = pl.ds(pl.multiple_of(r * HALF, HALF), HALF)
    other_cols = pl.ds(pl.multiple_of((1 - r) * HALF, HALF), HALF)

    def load(k):
        return pltpu.make_async_copy(proto.at[pl.ds(k * HALF, HALF), my_cols], stage.at[k % 2], ld_sem.at[k])

    load(0).start()
    load(1).start()
    designs_in = [
        pltpu.make_async_copy(des.at[:, my_cols], des_m, des_sem.at[0]),
        pltpu.make_async_copy(des.at[:, other_cols], des_o, des_sem.at[1]),
    ]
    for c in designs_in:
        c.start()

    barrier = pltpu.get_barrier_semaphore()
    partners = [sibling]
    for k in (1, 2, 3):
        partners += [along_v(k, r), along_v(k, 1 - r), along_u(k, 1 - r), (p, ((y + k) % SIDE) * 2 + r)]
    partners += [along_u(1, r), along_u(3, r)]
    for q in partners:
        pl.semaphore_signal(barrier, inc=1, device_id=q, device_id_type=MESH)

    row = cand[...]
    col = to_column(row)
    same = (row >> 4) == (col >> 4)
    rank = jnp.sum(jnp.where(same & (iota((CANDS, CANDS), 1) < iota((CANDS, CANDS), 0)), 1, 0), axis=1, keepdims=True)
    slot = (col >> 4) * 2 + rank
    hit = slot == iota((CANDS, TILE), 1)
    wanted = jnp.sum(jnp.where(hit, (col & 15) + 1, 0), axis=0, keepdims=True) - 1
    req_v[...] = jnp.broadcast_to(wanted, (8, TILE))
    block = pos[...] >> 7
    spot = jnp.sum(jnp.where(col == block, slot, 0), axis=0, keepdims=True)
    prow[...] = spot * TILE + (pos[...] & 127)
    pltpu.make_async_copy(req_v, req_own, own_sem).start()

    pl.semaphore_wait(barrier, len(partners))

    req_in[0] = req_v[...]
    requests = [remote(req_v, req_in.at[1], rq_s.at[0], rq_r.at[1], sibling)]
    for k in (1, 2, 3):
        back = (SIDE - k) * 2
        requests.append(remote(req_v, req_in.at[back], rq_s.at[2 * k - 1], rq_r.at[back], along_v(k, r)))
        requests.append(remote(req_v, req_in.at[back + 1], rq_s.at[2 * k], rq_r.at[back + 1], along_u(k, 1 - r)))
    for c in requests:
        c.start()

    def own_chunk(k, way):
        part = pl.ds(4 * k, 4)
        dst = tab3 if way == 0 else tab1
        return remote(tab0.at[part], dst.at[part], ag_s.at[way, k], ag_r.at[way, k], along_u(1 if way == 0 else 3, r))

    for k in range(4):
        load(k).wait()
        for b in range(4):
            tab0[4 * k + b] = stage[k % 2, TILE * b : TILE * (b + 1)].astype(BF16)
        own_chunk(k, 0).start()
        own_chunk(k, 1).start()
        if k < 2:
            load(k + 2).start()

    for c in designs_in:
        c.wait()

    @pl.loop(0, 4)
    def _(i):
        part = pl.ds(pl.multiple_of(i * COLS, COLS), COLS)
        dt_m[:, part] = des_m[part, :].T
        dt_o[:, part] = des_o[part, :].T

    for n in range(1, 8):
        remote(req_v, req_in.at[n], rq_s.at[0], rq_r.at[n], sibling).wait_recv()
    to_scalars = pltpu.make_async_copy(req_in, req_s, loc_sem.at[0])
    to_scalars.start()
    to_scalars.wait()

    def wanted_blocks(ku):
        first = owner(ku, 0) * 2
        for n in range(8):
            k, so = n // 2, n % 2
            for i in range(2):
                val = tab[ku][jnp.maximum(req_s[n, 0, first + i], 0)]
                if n == 0:
                    arr_m[0, ku, i] = val
                else:
                    send[n, ku, i] = val
            if n:
                fetched(n, ku).start()

    def fetched(n, ku):
        k, so = n // 2, n % 2
        back = (SIDE - k) % SIDE
        if so == 0:
            return remote(send.at[n, ku], arr_m.at[back, ku], f_s.at[n, ku], fm_r.at[back, ku], along_v(k, r))
        return remote(send.at[n, ku], arr_o.at[back, ku], f_s.at[n, ku], fo_r.at[back, ku], along_v(k, 1 - r))

    def relay(k):
        part = pl.ds(4 * k, 4)
        src, to = (tab3, 1) if k < 2 else (tab1, 3)
        return remote(src.at[part], tab2.at[part], rl_s.at[k], rl_r.at[k], along_u(to, r))

    def pass_on(k):
        own_chunk(k, 0 if k < 2 else 1).wait_recv()
        relay(k).start()

    pass_on(0)
    wanted_blocks(0)
    pass_on(1)
    own_chunk(0, 1).wait_recv()
    own_chunk(1, 1).wait_recv()
    pass_on(2)
    own_chunk(2, 0).wait_recv()
    pass_on(3)
    own_chunk(3, 0).wait_recv()
    wanted_blocks(1)
    wanted_blocks(3)
    for k in range(4):
        relay(k).wait_recv()
    wanted_blocks(2)

    for ku in range(4):
        first = owner(ku, 0) * 2
        eye = iota((8, TILE), 1)
        reqs = req_in[:, 0, :]
        ids = [jnp.sum(jnp.where(eye == first + i, reqs, 0), axis=1, keepdims=True) for i in range(2)]
        ids = jnp.concatenate(ids, axis=0)
        place = iota((BLOCKS, 1), 0)
        entry = (place % 8) * 2 + place // 8
        key = ids * BLOCKS + entry
        rank = jnp.sum(jnp.where(to_row(key) < key, 1, 0), axis=1, keepdims=True)
        at = rank == iota((BLOCKS, TILE), 1)
        follows = jnp.sum(jnp.where((to_row(key) < key) & (to_row(ids) == ids), 1, 0), axis=1, keepdims=True)
        lane = iota((BLOCKS, TILE), 1)
        rows = [
            jnp.sum(jnp.where(at, entry, 0), axis=0, keepdims=True),
            jnp.sum(jnp.where(at & (follows == 0), 1, 0), axis=0, keepdims=True),
            jnp.maximum(jnp.sum(jnp.where(ids <= lane, 1, 0), axis=0, keepdims=True) - 1, 0),
            jnp.sum(jnp.where(ids == lane, 1, 0), axis=0, keepdims=True),
        ]
        for i in range(4):
            order_v[ku, i : i + 1, :] = rows[i]
    order_copy = pltpu.make_async_copy(order_v, order_s, loc_sem.at[1])
    order_copy.start()
    pltpu.make_async_copy(req_v, req_own, own_sem).wait()

    def logits_of(ku, kv, part):
        o = owner(ku, kv)
        left = jnp.dot(arr_m[kv, ku].reshape(PAIR, HALF), dt_m[:, part], preferred_element_type=F32)
        right = jnp.dot(arr_o[ku, kv].reshape(PAIR, HALF), dt_o[:, part], preferred_element_type=F32)
        rows = iota((PAIR, COLS), 0)
        held = jnp.where(rows < TILE, req_own[0, o * 2], req_own[0, o * 2 + 1]) >= 0
        target = rows + o * PAIR == prow[:, part]
        return jnp.where(held, (left + right) * D**-0.5, LOW), target

    m_run[...] = jnp.full((1, ROWS), LOW, F32)
    s_run[...] = jnp.zeros((1, ROWS), F32)
    pick[...] = jnp.zeros((1, ROWS), F32)

    @pl.loop(0, 16)
    def _(n):
        ku, kv = pair_of(n)

        @pl.when(kv != 0)
        def _():
            remote(send.at[1, 0], arr_m.at[kv, ku], f_s.at[1, 0], fm_r.at[kv, ku], sibling).wait_recv()

        remote(send.at[1, 0], arr_o.at[ku, kv], f_s.at[1, 0], fo_r.at[ku, kv], sibling).wait_recv()

        @pl.loop(0, ROWS // COLS)
        def _(i):
            part = pl.ds(pl.multiple_of(i * COLS, COLS), COLS)
            logits, target = logits_of(ku, kv, part)
            pick[:, part] += jnp.sum(jnp.where(target, logits, 0.0), axis=0, keepdims=True)
            before = m_run[:, part]
            now = jnp.maximum(before, jnp.max(logits, axis=0, keepdims=True))
            m_run[:, part] = now
            s_run[:, part] = s_run[:, part] * jnp.exp(before - now) + jnp.sum(jnp.exp(logits - now), axis=0, keepdims=True)

    total[...] = m_run[...] + jnp.log(s_run[...])
    loss_o[...] = total[...] - pick[...]

    for n in range(1, 8):
        for ku in range(4):
            fetched(n, ku).wait_send()
    for c in requests:
        c.wait_send()
    for k in range(4):
        own_chunk(k, 0).wait_send()
        own_chunk(k, 1).wait_send()
        relay(k).wait_send()

    def back_mine(ku, kv, k):
        back = (SIDE - kv) % SIDE
        return remote(send.at[kv * 2, ku], rr[k].at[pl.ds(back * 4, 2)], b_s.at[kv * 2, ku], b_r.at[k, back, 0], along_v(kv, r))

    def back_other(ku, kv, k):
        back = (SIDE - ku) % SIDE
        return remote(send.at[ku * 2 + 1, kv], rr[k].at[pl.ds(back * 4 + 2, 2)], b_s.at[ku * 2 + 1, kv], b_r.at[k, back, 1], along_u(ku, 1 - r))

    @pl.loop(0, 16)
    def _(n):
        ku, kv = pair_of(15 - n)

        @pl.loop(0, ROWS // COLS)
        def _(i):
            part = pl.ds(pl.multiple_of(i * COLS, COLS), COLS)
            logits, target = logits_of(ku, kv, part)
            grads[kv, ku, :, part] = (jnp.exp(logits - total[:, part]) - jnp.where(target, 1.0, 0.0)).astype(BF16)

        mine = jnp.dot(grads[kv, ku], des_m[...], preferred_element_type=F32).astype(BF16).reshape(2, TILE, HALF)
        send[kv * 2, ku] = mine
        other = jnp.dot(grads[kv, ku], des_o[...], preferred_element_type=F32).astype(BF16).reshape(2, TILE, HALF)
        send[ku * 2 + 1, kv] = other
        for k in range(4):

            @pl.when(ku == k)
            def _():
                @pl.when(kv == 0)
                def _():
                    rr[k][0:2] = send[0, k]

                @pl.when(kv != 0)
                def _():
                    back_mine(ku, kv, k).start()

            @pl.when(kv == k)
            def _():
                back_other(ku, kv, k).start()

    order_copy.wait()

    def sums(ku):
        for n in range(1, 8):
            k, so = n // 2, n % 2
            remote(send.at[1, 0], rr[ku].at[pl.ds(2 * n, 2)], b_s.at[1, 0], b_r.at[ku, k, so], sibling).wait_recv()

        @pl.loop(0, TILE // 16)
        def _(i):
            part = pl.ds(pl.multiple_of(i * 16, 16), 16)
            acc = jnp.zeros((16, HALF), F32)
            for t in range(BLOCKS):
                val = rr[ku][order_s[ku, 0, t], part, :].astype(F32)
                acc = jnp.where(order_s[ku, 1, t] == 1, val, acc + val)
                runs[t] = acc
            for j in range(BLOCKS):
                val = runs[order_s[ku, 2, j]]
                tab[ku][j, part, :] = jnp.where(order_s[ku, 3, j] > 0, val, 0.0).astype(BF16)

    def design_grad(q):
        part = pl.ds(q * COLS, COLS)
        for h in range(2):
            acc = stage.at[0, pl.ds(0, COLS)]
            acc[...] = jnp.zeros((COLS, HALF), F32)

            @pl.loop(0, 4)
            def _(k):
                lhs = grads[k, :, :, part] if h == 0 else grads[:, k, :, part]
                rhs = arr_m[k] if h == 0 else arr_o[k]
                acc[...] += lax.dot_general(
                    lhs.reshape(ROWS, COLS), rhs.reshape(ROWS, HALF), (((0,), (0,)), ((), ())), preferred_element_type=F32
                )

            dg_s[q, h] = acc[...].astype(BF16)
            dg_out(q, h).start()

    def dg_out(q, h):
        cols = my_cols if h == 0 else other_cols
        return pltpu.make_async_copy(dg_s.at[q, h], dg_o.at[pl.ds(q * COLS, COLS), cols], out_sem.at[q, h])

    def far(g):
        part = pl.ds(4 * g, 4)
        return remote(tab2.at[part], merge.at[g], mg_s.at[g], mg_r.at[g], along_u(1 if g < 2 else 3, r))

    def near(g, way):
        part = pl.ds(4 * g, 4)
        if way == 0:
            return remote(tab1.at[part], from_down.at[g], rs_s.at[0, g], rs_r.at[0, g], along_u(1, r))
        return remote(tab3.at[part], from_up.at[g], rs_s.at[1, g], rs_r.at[1, g], along_u(3, r))

    def merged(g):
        src = tab1 if g < 2 else tab3
        far(g).wait_recv()
        for b in range(4):
            src[4 * g + b] = (src[4 * g + b].astype(F32) + merge[g, b].astype(F32)).astype(BF16)
        near(g, 0 if g < 2 else 1).start()

    sums(2)
    for g in (0, 2, 1, 3):
        far(g).start()
    design_grad(0)
    sums(1)
    near(2, 0).start()
    near(3, 0).start()
    sums(3)
    near(0, 1).start()
    near(1, 1).start()
    for g in (0, 2, 1, 3):
        merged(g)
    sums(0)
    design_grad(1)
    design_grad(2)

    def to_y(g):
        return remote(tab0.at[pl.ds(4 * g, 4)], from_y.at[(y - g + SIDE) % SIDE], y_s.at[g], y_r.at[(y - g + SIDE) % SIDE], (p, g * 2 + r))

    for g in (0, 2, 1, 3):
        near(g, 0).wait_recv()
        near(g, 1).wait_recv()
        for b in range(4):
            val = tab0[4 * g + b].astype(F32) + from_up[g, b].astype(F32) + from_down[g, b].astype(F32)
            tab0[4 * g + b] = val.astype(BF16)

        @pl.when(y != g)
        def _():
            to_y(g).start()

    design_grad(3)
    for k in (1, 3, 2):
        remote(tab0.at[pl.ds(0, 4)], from_y.at[k], y_s.at[0], y_r.at[k], sibling).wait_recv()

    def reduced(b):
        val = tab0[4 * y + b].astype(F32)
        for k in (1, 2, 3):
            val += from_y[k, b].astype(F32)
        return val

    for i in range(2):
        stage[1, pl.ds(PAIR + i * TILE, TILE)] = reduced(2 * (1 - r) + i)
    cross = remote(stage.at[1, pl.ds(PAIR, PAIR)], core_in, c_s, c_r, sibling)
    cross.start()
    for i in range(2):
        stage[1, pl.ds(i * TILE, TILE)] = reduced(2 * r + i)
    outs = [pltpu.make_async_copy(stage.at[1, pl.ds(0, PAIR)], pg_o.at[:, my_cols], loc_sem.at[2])]
    outs[0].start()
    cross.wait_recv()
    outs.append(pltpu.make_async_copy(core_in, pg_o.at[:, other_cols], loc_sem.at[3]))
    outs[1].start()

    for kv in range(4):
        for ku in range(4):
            if kv:
                back_mine(ku, kv, ku).wait_send()
            back_other(ku, kv, kv).wait_send()
    for g in range(4):
        far(g).wait_send()
        near(g, 0).wait_send()
        near(g, 1).wait_send()

        @pl.when(y != g)
        def _():
            to_y(g).wait_send()

        for h in range(2):
            dg_out(g, h).wait()
    cross.wait_send()
    for c in outs:
        c.wait()


def body(designs, prototypes, candidates, positives):
    vmem = lambda shape, dtype: pltpu.VMEM(shape, dtype)
    dma = lambda *shape: pltpu.SemaphoreType.DMA(shape)
    blocks = (BLOCKS, TILE, HALF)
    pairs = (SIDE, SIDE, 2, TILE, HALF)
    losses, design_grad, proto_grad = pl.pallas_call(
        kernel,
        out_shape=(
            jax.ShapeDtypeStruct((1, ROWS), F32),
            jax.ShapeDtypeStruct((ROWS, D), BF16),
            jax.ShapeDtypeStruct((PAIR, D), F32),
        ),
        in_specs=[
            pl.BlockSpec(memory_space=pl.ANY),
            pl.BlockSpec(memory_space=pl.ANY),
            pl.BlockSpec(memory_space=pltpu.VMEM),
            pl.BlockSpec(memory_space=pltpu.VMEM),
        ],
        out_specs=(
            pl.BlockSpec(memory_space=pltpu.VMEM),
            pl.BlockSpec(memory_space=pl.ANY),
            pl.BlockSpec(memory_space=pl.ANY),
        ),
        scratch_shapes=[
            *[vmem(blocks, BF16) for _ in range(8)],
            vmem((8, SIDE, 2, TILE, HALF), BF16),
            vmem(pairs, BF16),
            vmem(pairs, BF16),
            vmem((ROWS, HALF), BF16),
            vmem((ROWS, HALF), BF16),
            vmem((HALF, ROWS), BF16),
            vmem((HALF, ROWS), BF16),
            vmem((SIDE, SIDE, PAIR, ROWS), BF16),
            vmem((2, HALF, HALF), F32),
            vmem((4, 4, TILE, HALF), BF16),
            vmem((4, 4, TILE, HALF), BF16),
            vmem((4, 4, TILE, HALF), BF16),
            vmem((4, 4, TILE, HALF), BF16),
            vmem((BLOCKS, 16, HALF), F32),
            vmem((PAIR, HALF), F32),
            vmem((4, 2, COLS, HALF), BF16),
            vmem((1, ROWS), I32),
            *[vmem((1, ROWS), F32) for _ in range(4)],
            vmem((8, TILE), I32),
            vmem((8, 8, TILE), I32),
            vmem((4, 8, TILE), I32),
            pltpu.SMEM((8, TILE), I32),
            pltpu.SMEM((8, 8, TILE), I32),
            pltpu.SMEM((4, 8, TILE), I32),
            dma(4),
            dma(2),
            dma(4, 2),
            dma(4),
            pltpu.SemaphoreType.DMA,
            dma(8),
            dma(8),
            dma(2, 4),
            dma(2, 4),
            dma(4),
            dma(4),
            dma(8, 4),
            dma(4, 4),
            dma(4, 4),
            dma(8, 4),
            dma(4, 4, 2),
            dma(4),
            dma(4),
            dma(2, 4),
            dma(2, 4),
            dma(4),
            dma(4),
            pltpu.SemaphoreType.DMA,
            pltpu.SemaphoreType.DMA,
        ],
        compiler_params=pltpu.CompilerParams(
            collective_id=0, has_side_effects=True, vmem_limit_bytes=62 * 2**20
        ),
    )(designs, prototypes, candidates, positives.reshape(1, ROWS))
    return losses.reshape(ROWS), design_grad, proto_grad


def solution(mesh):
    return jax.shard_map(
        body,
        mesh=mesh,
        in_specs=(
            P(("proto", "design"), None),
            P("proto", None),
            P(("proto", "design"), None),
            P(("proto", "design")),
        ),
        out_specs=(
            P(("proto", "design")),
            P(("proto", "design"), None),
            P(("proto", "design"), None),
        ),
        check_vma=False,
    )
```

```python
import jax
import jax.numpy as jnp
from jax import lax
from jax.experimental import pallas as pl
from jax.experimental.pallas import tpu as pltpu
from jax.sharding import PartitionSpec as P

D = 1024
HALF = 512
TILE = 128
ROWS = 1024
SIDE = 4
BLOCKS = 16
CANDS = 24
PAIR = 2 * TILE
COLS = 256
LOW = -3.0e38
MESH = pl.DeviceIdType.MESH
BF16 = jnp.bfloat16
F32 = jnp.float32
I32 = jnp.int32


def remote(src, dst, send_sem, recv_sem, device):
    return pltpu.make_async_remote_copy(
        src_ref=src, dst_ref=dst, send_sem=send_sem, recv_sem=recv_sem, device_id=device, device_id_type=MESH
    )


def iota(shape, dim):
    return lax.broadcasted_iota(I32, shape, dim)


def to_column(row):
    n = row.shape[1]
    return jnp.sum(jnp.where(iota((n, n), 0) == iota((n, n), 1), jnp.broadcast_to(row, (n, n)), 0), axis=1, keepdims=True)


def to_row(col):
    n = col.shape[0]
    return jnp.sum(jnp.where(iota((n, n), 0) == iota((n, n), 1), jnp.broadcast_to(col, (n, n)), 0), axis=0, keepdims=True)


def gray(k):
    return k + (k // 2) * (1 - 2 * (k % 2))


def pair_of(n):
    s = jnp.where(n >= 1, 1, 0) + jnp.where(n >= 4, 1, 0) + jnp.where(n >= 9, 1, 0)
    m = n - s * s
    odd = m % 2
    return gray(s + odd * (m // 2 - s)), gray(m // 2 + odd * (s - m // 2))


def kernel(
    des, proto, cand, pos, loss_o, dg_o, pg_o,
    tab0, tab1, tab2, tab3, rr0, rr1, rr2, rr3,
    send, arr_m, arr_o, des_m, des_o, dt_m, dt_o, grads, stage, merge, from_up, from_down, from_y, far_y, runs, core_in, dg_s,
    prow, m_run, s_run, pick, total, req_v, req_in, order_v, req_own, req_s, order_s,
    ld_sem, des_sem, out_sem, loc_sem, own_sem, rq_s, rq_r, ag_s, ag_r, rl_s, rl_r, gy_s, gy_r, f_s, fm_r, fo_r, b_s, b_r,
    fy_s, fy_r, mg_s, mg_r, rs_s, rs_r, y_s, y_r, c_s, c_r,
):
    p, d = lax.axis_index("proto"), lax.axis_index("design")
    x, z, y, r = p // SIDE, p % SIDE, d // 2, d % 2
    tab, rr = (tab0, tab1, tab2, tab3), (rr0, rr1, rr2, rr3)

    def owner(ku, kv):
        return ((x + ku * (1 - r) + kv * r) % SIDE) * SIDE + (z + ku * r + kv * (1 - r)) % SIDE

    def along_u(k, core):
        return (owner(k, 0), y * 2 + core)

    def along_v(k, core):
        return (owner(0, k), y * 2 + core)

    def along_y(k):
        return (p, ((y + k) % SIDE) * 2 + r)

    def group(k):
        return pl.ds(((y + k) % SIDE) * 4, 4)

    sibling = (p, y * 2 + 1 - r)
    my_cols = pl.ds(pl.multiple_of(r * HALF, HALF), HALF)
    other_cols = pl.ds(pl.multiple_of((1 - r) * HALF, HALF), HALF)

    def load(k):
        rows = pl.ds(pl.multiple_of(((y + k) % SIDE) * HALF, HALF), HALF)
        return pltpu.make_async_copy(proto.at[rows, my_cols], stage.at[k % 2], ld_sem.at[k])

    load(0).start()
    load(1).start()
    designs_in = [
        pltpu.make_async_copy(des.at[:, my_cols], des_m, des_sem.at[0]),
        pltpu.make_async_copy(des.at[:, other_cols], des_o, des_sem.at[1]),
    ]
    for c in designs_in:
        c.start()

    barrier = pltpu.get_barrier_semaphore()
    partners = [sibling]
    for k in (1, 2, 3):
        partners += [along_v(k, r), along_v(k, 1 - r), along_u(k, 1 - r), along_y(k)]
    partners += [along_u(1, r), along_u(3, r)]
    for q in partners:
        pl.semaphore_signal(barrier, inc=1, device_id=q, device_id_type=MESH)

    row = cand[...]
    col = to_column(row)
    same = (row >> 4) == (col >> 4)
    rank = jnp.sum(jnp.where(same & (iota((CANDS, CANDS), 1) < iota((CANDS, CANDS), 0)), 1, 0), axis=1, keepdims=True)
    slot = (col >> 4) * 2 + rank
    hit = slot == iota((CANDS, TILE), 1)
    wanted = jnp.sum(jnp.where(hit, (col & 15) + 1, 0), axis=0, keepdims=True) - 1
    req_v[...] = jnp.broadcast_to(wanted, (8, TILE))
    block = pos[...] >> 7
    spot = jnp.sum(jnp.where(col == block, slot, 0), axis=0, keepdims=True)
    prow[...] = spot * TILE + (pos[...] & 127)
    pltpu.make_async_copy(req_v, req_own, own_sem).start()

    pl.semaphore_wait(barrier, len(partners))

    req_in[0] = req_v[...]
    requests = [remote(req_v, req_in.at[1], rq_s.at[0], rq_r.at[1], sibling)]
    for k in (1, 2, 3):
        back = (SIDE - k) * 2
        requests.append(remote(req_v, req_in.at[back], rq_s.at[2 * k - 1], rq_r.at[back], along_v(k, r)))
        requests.append(remote(req_v, req_in.at[back + 1], rq_s.at[2 * k], rq_r.at[back + 1], along_u(k, 1 - r)))
    for c in requests:
        c.start()

    def own_chunk(k, way):
        part = group(k)
        dst = tab3 if way == 0 else tab1
        return remote(tab0.at[part], dst.at[part], ag_s.at[way, k], ag_r.at[way, k], along_u(1 if way == 0 else 3, r))

    for k in range(4):
        load(k).wait()
        for b in range(4):
            tab0[((y + k) % SIDE) * 4 + b] = stage[k % 2, TILE * b : TILE * (b + 1)].astype(BF16)
        if k < 2:
            own_chunk(k, 0).start()
            own_chunk(k, 1).start()
            load(k + 2).start()

    for c in designs_in:
        c.wait()

    @pl.loop(0, 4)
    def _(i):
        part = pl.ds(pl.multiple_of(i * COLS, COLS), COLS)
        dt_m[:, part] = des_m[part, :].T
        dt_o[:, part] = des_o[part, :].T

    for n in range(1, 8):
        remote(req_v, req_in.at[n], rq_s.at[0], rq_r.at[n], sibling).wait_recv()
    to_scalars = pltpu.make_async_copy(req_in, req_s, loc_sem.at[0])
    to_scalars.start()
    to_scalars.wait()

    def wanted_blocks(ku):
        first = owner(ku, 0) * 2
        for n in (0, 2, 3, 6, 7, 1, 4, 5):
            for i in range(2):
                val = tab[ku][jnp.maximum(req_s[n, 0, first + i], 0)]
                if n == 0:
                    arr_m[0, ku, i] = val
                else:
                    send[n, ku, i] = val
            if n:
                fetched(n, ku).start()

    def fetched(n, ku):
        k, so = n // 2, n % 2
        back = (SIDE - k) % SIDE
        if so == 0:
            return remote(send.at[n, ku], arr_m.at[back, ku], f_s.at[n, ku], fm_r.at[back, ku], along_v(k, r))
        return remote(send.at[n, ku], arr_o.at[back, ku], f_s.at[n, ku], fo_r.at[back, ku], along_v(k, 1 - r))

    def relay(way):
        part = pl.ds(4 * y + 2 * way, 2)
        src, to = (tab3, 1) if way == 0 else (tab1, 3)
        return remote(src.at[part], tab2.at[part], rl_s.at[way], rl_r.at[way], along_u(to, r))

    def share(k):
        return remote(tab2.at[group(0)], tab2.at[group(0)], gy_s.at[k], gy_r.at[SIDE - k], along_y(k))

    for way in (0, 1):
        own_chunk(0, way).wait_recv()
        relay(way).start()
    for k in (2, 3):
        own_chunk(k, 0).start()
        own_chunk(k, 1).start()
    for way in (0, 1):
        relay(way).wait_recv()
    for k in (1, 3, 2):
        share(k).start()
    wanted_blocks(0)
    for k in (1, 2, 3):
        own_chunk(k, 1).wait_recv()
    wanted_blocks(1)
    for k in (1, 2, 3):
        own_chunk(k, 0).wait_recv()
    wanted_blocks(3)
    for k in (1, 2, 3):
        remote(tab2.at[group(0)], tab2.at[group(0)], gy_s.at[k], gy_r.at[k], sibling).wait_recv()
    wanted_blocks(2)

    for ku in range(4):
        first = owner(ku, 0) * 2
        eye = iota((8, TILE), 1)
        reqs = req_in[:, 0, :]
        ids = [jnp.sum(jnp.where(eye == first + i, reqs, 0), axis=1, keepdims=True) for i in range(2)]
        ids = jnp.concatenate(ids, axis=0)
        place = iota((BLOCKS, 1), 0)
        entry = (place % 8) * 2 + place // 8
        key = ids * BLOCKS + entry
        rank = jnp.sum(jnp.where(to_row(key) < key, 1, 0), axis=1, keepdims=True)
        at = rank == iota((BLOCKS, TILE), 1)
        follows = jnp.sum(jnp.where((to_row(key) < key) & (to_row(ids) == ids), 1, 0), axis=1, keepdims=True)
        lane = iota((BLOCKS, TILE), 1)
        rows = [
            jnp.sum(jnp.where(at, entry, 0), axis=0, keepdims=True),
            jnp.sum(jnp.where(at & (follows == 0), 1, 0), axis=0, keepdims=True),
            jnp.maximum(jnp.sum(jnp.where(ids <= lane, 1, 0), axis=0, keepdims=True) - 1, 0),
            jnp.sum(jnp.where(ids == lane, 1, 0), axis=0, keepdims=True),
        ]
        for i in range(4):
            order_v[ku, i : i + 1, :] = rows[i]
    order_copy = pltpu.make_async_copy(order_v, order_s, loc_sem.at[1])
    order_copy.start()
    pltpu.make_async_copy(req_v, req_own, own_sem).wait()

    def logits_of(ku, kv, part):
        o = owner(ku, kv)
        left = jnp.dot(arr_m[kv, ku].reshape(PAIR, HALF), dt_m[:, part], preferred_element_type=F32)
        right = jnp.dot(arr_o[ku, kv].reshape(PAIR, HALF), dt_o[:, part], preferred_element_type=F32)
        rows = iota((PAIR, COLS), 0)
        held = jnp.where(rows < TILE, req_own[0, o * 2], req_own[0, o * 2 + 1]) >= 0
        target = rows + o * PAIR == prow[:, part]
        return jnp.where(held, (left + right) * D**-0.5, LOW), target

    m_run[...] = jnp.full((1, ROWS), LOW, F32)
    s_run[...] = jnp.zeros((1, ROWS), F32)
    pick[...] = jnp.zeros((1, ROWS), F32)

    @pl.loop(0, 16)
    def _(n):
        ku, kv = pair_of(n)

        @pl.when(kv != 0)
        def _():
            remote(send.at[1, 0], arr_m.at[kv, ku], f_s.at[1, 0], fm_r.at[kv, ku], sibling).wait_recv()

        remote(send.at[1, 0], arr_o.at[ku, kv], f_s.at[1, 0], fo_r.at[ku, kv], sibling).wait_recv()

        @pl.loop(0, ROWS // COLS)
        def _(i):
            part = pl.ds(pl.multiple_of(i * COLS, COLS), COLS)
            logits, target = logits_of(ku, kv, part)
            pick[:, part] += jnp.sum(jnp.where(target, logits, 0.0), axis=0, keepdims=True)
            before = m_run[:, part]
            now = jnp.maximum(before, jnp.max(logits, axis=0, keepdims=True))
            m_run[:, part] = now
            s_run[:, part] = s_run[:, part] * jnp.exp(before - now) + jnp.sum(jnp.exp(logits - now), axis=0, keepdims=True)

    total[...] = m_run[...] + jnp.log(s_run[...])
    loss_o[...] = total[...] - pick[...]

    for n in range(1, 8):
        for ku in range(4):
            fetched(n, ku).wait_send()
    for c in requests:
        c.wait_send()
    for k in range(4):
        own_chunk(k, 0).wait_send()
        own_chunk(k, 1).wait_send()
    for way in (0, 1):
        relay(way).wait_send()
    for k in (1, 2, 3):
        share(k).wait_send()

    def back_mine(ku, kv, k):
        back = (SIDE - kv) % SIDE
        return remote(send.at[kv * 2, ku], rr[k].at[pl.ds(back * 4, 2)], b_s.at[kv * 2, ku], b_r.at[k, back, 0], along_v(kv, r))

    def back_other(ku, kv, k):
        back = (SIDE - ku) % SIDE
        return remote(send.at[ku * 2 + 1, kv], rr[k].at[pl.ds(back * 4 + 2, 2)], b_s.at[ku * 2 + 1, kv], b_r.at[k, back, 1], along_u(ku, 1 - r))

    @pl.loop(0, 16)
    def _(n):
        ku, kv = pair_of(15 - n)

        @pl.loop(0, ROWS // COLS)
        def _(i):
            part = pl.ds(pl.multiple_of(i * COLS, COLS), COLS)
            logits, target = logits_of(ku, kv, part)
            grads[kv, ku, :, part] = (jnp.exp(logits - total[:, part]) - jnp.where(target, 1.0, 0.0)).astype(BF16)

        mine = jnp.dot(grads[kv, ku], des_m[...], preferred_element_type=F32).astype(BF16).reshape(2, TILE, HALF)
        send[kv * 2, ku] = mine
        other = jnp.dot(grads[kv, ku], des_o[...], preferred_element_type=F32).astype(BF16).reshape(2, TILE, HALF)
        send[ku * 2 + 1, kv] = other
        for k in range(4):

            @pl.when(ku == k)
            def _():
                @pl.when(kv == 0)
                def _():
                    rr[k][0:2] = send[0, k]

                @pl.when(kv != 0)
                def _():
                    back_mine(ku, kv, k).start()

            @pl.when(kv == k)
            def _():
                back_other(ku, kv, k).start()

    order_copy.wait()

    def sums(ku):
        for n in range(1, 8):
            k, so = n // 2, n % 2
            remote(send.at[1, 0], rr[ku].at[pl.ds(2 * n, 2)], b_s.at[1, 0], b_r.at[ku, k, so], sibling).wait_recv()

        @pl.loop(0, TILE // 16)
        def _(i):
            part = pl.ds(pl.multiple_of(i * 16, 16), 16)
            acc = jnp.zeros((16, HALF), F32)
            for t in range(BLOCKS):
                val = rr[ku][order_s[ku, 0, t], part, :].astype(F32)
                acc = jnp.where(order_s[ku, 1, t] == 1, val, acc + val)
                runs[t] = acc
            for j in range(BLOCKS):
                val = runs[order_s[ku, 2, j]]
                tab[ku][j, part, :] = jnp.where(order_s[ku, 3, j] > 0, val, 0.0).astype(BF16)

    def design_grad(q, h):
        part = pl.ds(q * COLS, COLS)
        acc = stage.at[0, pl.ds(0, COLS)]
        acc[...] = jnp.zeros((COLS, HALF), F32)

        @pl.loop(0, 4)
        def _(k):
            lhs = grads[k, :, :, part] if h == 0 else grads[:, k, :, part]
            rhs = arr_m[k] if h == 0 else arr_o[k]
            acc[...] += lax.dot_general(
                lhs.reshape(ROWS, COLS), rhs.reshape(ROWS, HALF), (((0,), (0,)), ((), ())), preferred_element_type=F32
            )

        dg_s[q, h] = acc[...].astype(BF16)
        dg_out(q, h).start()

    def dg_out(q, h):
        cols = my_cols if h == 0 else other_cols
        return pltpu.make_async_copy(dg_s.at[q, h], dg_o.at[pl.ds(q * COLS, COLS), cols], out_sem.at[q, h])

    def far_along_y(k):
        return remote(tab2.at[group(k)], far_y.at[SIDE - k], fy_s.at[k], fy_r.at[SIDE - k], along_y(k))

    def far(way):
        part = pl.ds(4 * y + 2 * way, 2)
        return remote(tab2.at[part], merge.at[way], mg_s.at[way], mg_r.at[way], along_u(1 if way == 0 else 3, r))

    def near(k, way):
        if way == 0:
            return remote(tab1.at[group(k)], from_down.at[k], rs_s.at[0, k], rs_r.at[0, k], along_u(1, r))
        return remote(tab3.at[group(k)], from_up.at[k], rs_s.at[1, k], rs_r.at[1, k], along_u(3, r))

    def to_y(k):
        return remote(tab0.at[group(k)], from_y.at[SIDE - k], y_s.at[k], y_r.at[SIDE - k], along_y(k))

    sums(2)
    for k in (1, 3, 2):
        far_along_y(k).start()
    design_grad(0, 0)
    design_grad(0, 1)
    design_grad(1, 0)
    sums(3)
    for k in (1, 3, 2):
        near(k, 1).start()
    sums(1)
    for k in (1, 3, 2):
        near(k, 0).start()
    sums(0)
    design_grad(1, 1)
    design_grad(2, 0)
    for k in (1, 3, 2):
        remote(tab2.at[group(0)], far_y.at[k], fy_s.at[k], fy_r.at[k], sibling).wait_recv()
    for b in range(4):
        val = tab2[4 * y + b].astype(F32)
        for k in (1, 2, 3):
            val += far_y[k, b].astype(F32)
        tab2[4 * y + b] = val.astype(BF16)
    far(0).start()
    far(1).start()

    def add_near(k):
        near(k, 0).wait_recv()
        near(k, 1).wait_recv()
        for b in range(4):
            at = ((y + k) % SIDE) * 4 + b
            val = tab0[at].astype(F32) + from_up[k, b].astype(F32) + from_down[k, b].astype(F32)
            tab0[at] = val.astype(BF16)

    add_near(1)
    to_y(1).start()
    for way in (0, 1):
        src = tab1 if way == 0 else tab3
        far(way).wait_recv()
        for b in range(2):
            at = 4 * y + 2 * way + b
            src[at] = (src[at].astype(F32) + merge[way, b].astype(F32)).astype(BF16)
        near(0, way).start()
    design_grad(2, 1)
    add_near(3)
    to_y(3).start()
    design_grad(3, 0)
    add_near(2)
    to_y(2).start()
    design_grad(3, 1)
    add_near(0)
    for k in (1, 3, 2):
        remote(tab0.at[pl.ds(0, 4)], from_y.at[k], y_s.at[0], y_r.at[k], sibling).wait_recv()

    def reduced(b):
        val = tab0[4 * y + b].astype(F32)
        for k in (1, 2, 3):
            val += from_y[k, b].astype(F32)
        return val

    for i in range(2):
        stage[1, pl.ds(PAIR + i * TILE, TILE)] = reduced(2 * (1 - r) + i)
    cross = remote(stage.at[1, pl.ds(PAIR, PAIR)], core_in, c_s, c_r, sibling)
    cross.start()
    for i in range(2):
        stage[1, pl.ds(i * TILE, TILE)] = reduced(2 * r + i)
    outs = [pltpu.make_async_copy(stage.at[1, pl.ds(0, PAIR)], pg_o.at[:, my_cols], loc_sem.at[2])]
    outs[0].start()
    cross.wait_recv()
    outs.append(pltpu.make_async_copy(core_in, pg_o.at[:, other_cols], loc_sem.at[3]))
    outs[1].start()

    for kv in range(4):
        for ku in range(4):
            if kv:
                back_mine(ku, kv, ku).wait_send()
            back_other(ku, kv, kv).wait_send()
    for k in range(4):
        near(k, 0).wait_send()
        near(k, 1).wait_send()
        if k:
            far_along_y(k).wait_send()
            to_y(k).wait_send()
        for h in range(2):
            dg_out(k, h).wait()
    far(0).wait_send()
    far(1).wait_send()
    cross.wait_send()
    for c in outs:
        c.wait()


def settle(losses, design_grad, proto_grad, losses_o, design_grad_o, proto_grad_o, one, many, few, sems):
    moves = [(losses, one, losses_o)]
    for i in range(4):
        part = pl.ds(i * COLS, COLS)
        moves.append((design_grad.at[part], many.at[part], design_grad_o.at[part]))
    for i in range(2):
        part = pl.ds(i * TILE, TILE)
        moves.append((proto_grad.at[part], few.at[part], proto_grad_o.at[part]))
    reads = [pltpu.make_async_copy(a, b, sems.at[0, n]) for n, (a, b, c) in enumerate(moves)]
    writes = [pltpu.make_async_copy(b, c, sems.at[1, n]) for n, (a, b, c) in enumerate(moves)]
    for c in reads:
        c.start()
    for a, b in zip(reads, writes):
        a.wait()
        b.start()
    for c in writes:
        c.wait()


def body(designs, prototypes, candidates, positives):
    vmem = lambda shape, dtype: pltpu.VMEM(shape, dtype)
    dma = lambda *shape: pltpu.SemaphoreType.DMA(shape)
    blocks = (BLOCKS, TILE, HALF)
    pairs = (SIDE, SIDE, 2, TILE, HALF)
    losses, design_grad, proto_grad = pl.pallas_call(
        kernel,
        out_shape=(
            jax.ShapeDtypeStruct((1, ROWS), F32),
            jax.ShapeDtypeStruct((ROWS, D), BF16),
            jax.ShapeDtypeStruct((PAIR, D), F32),
        ),
        in_specs=[
            pl.BlockSpec(memory_space=pl.ANY),
            pl.BlockSpec(memory_space=pl.ANY),
            pl.BlockSpec(memory_space=pltpu.VMEM),
            pl.BlockSpec(memory_space=pltpu.VMEM),
        ],
        out_specs=(
            pl.BlockSpec(memory_space=pltpu.VMEM),
            pl.BlockSpec(memory_space=pl.ANY),
            pl.BlockSpec(memory_space=pl.ANY),
        ),
        scratch_shapes=[
            *[vmem(blocks, BF16) for _ in range(8)],
            vmem((8, SIDE, 2, TILE, HALF), BF16),
            vmem(pairs, BF16),
            vmem(pairs, BF16),
            vmem((ROWS, HALF), BF16),
            vmem((ROWS, HALF), BF16),
            vmem((HALF, ROWS), BF16),
            vmem((HALF, ROWS), BF16),
            vmem((SIDE, SIDE, PAIR, ROWS), BF16),
            vmem((2, HALF, HALF), F32),
            vmem((2, 2, TILE, HALF), BF16),
            vmem((4, 4, TILE, HALF), BF16),
            vmem((4, 4, TILE, HALF), BF16),
            vmem((4, 4, TILE, HALF), BF16),
            vmem((4, 4, TILE, HALF), BF16),
            vmem((BLOCKS, 16, HALF), F32),
            vmem((PAIR, HALF), F32),
            vmem((4, 2, COLS, HALF), BF16),
            vmem((1, ROWS), I32),
            *[vmem((1, ROWS), F32) for _ in range(4)],
            vmem((8, TILE), I32),
            vmem((8, 8, TILE), I32),
            vmem((4, 8, TILE), I32),
            pltpu.SMEM((8, TILE), I32),
            pltpu.SMEM((8, 8, TILE), I32),
            pltpu.SMEM((4, 8, TILE), I32),
            dma(4),
            dma(2),
            dma(4, 2),
            dma(4),
            pltpu.SemaphoreType.DMA,
            dma(8),
            dma(8),
            dma(2, 4),
            dma(2, 4),
            dma(2),
            dma(2),
            dma(4),
            dma(4),
            dma(8, 4),
            dma(4, 4),
            dma(4, 4),
            dma(8, 4),
            dma(4, 4, 2),
            dma(4),
            dma(4),
            dma(2),
            dma(2),
            dma(2, 4),
            dma(2, 4),
            dma(4),
            dma(4),
            pltpu.SemaphoreType.DMA,
            pltpu.SemaphoreType.DMA,
        ],
        compiler_params=pltpu.CompilerParams(
            collective_id=0, has_side_effects=True, vmem_limit_bytes=62 * 2**20
        ),
    )(designs, prototypes, candidates, positives.reshape(1, ROWS))
    losses, design_grad, proto_grad = pl.pallas_call(
        settle,
        out_shape=(
            jax.ShapeDtypeStruct((1, ROWS), F32),
            jax.ShapeDtypeStruct((ROWS, D), BF16),
            jax.ShapeDtypeStruct((PAIR, D), F32),
        ),
        in_specs=[pl.BlockSpec(memory_space=pl.ANY)] * 3,
        out_specs=(pl.BlockSpec(memory_space=pl.ANY),) * 3,
        scratch_shapes=[vmem((1, ROWS), F32), vmem((ROWS, D), BF16), vmem((PAIR, D), F32), dma(2, 7)],
    )(losses, design_grad, proto_grad)
    return losses.reshape(ROWS), design_grad, proto_grad


def solution(mesh):
    return jax.shard_map(
        body,
        mesh=mesh,
        in_specs=(
            P(("proto", "design"), None),
            P("proto", None),
            P(("proto", "design"), None),
            P(("proto", "design")),
        ),
        out_specs=(
            P(("proto", "design")),
            P(("proto", "design"), None),
            P(("proto", "design"), None),
        ),
        check_vma=False,
    )
```

```python
import jax
import jax.numpy as jnp
from jax import lax
from jax.experimental import pallas as pl
from jax.experimental.pallas import tpu as pltpu
from jax.sharding import PartitionSpec as P

D = 1024
HALF = 512
TILE = 128
ROWS = 1024
SIDE = 4
BLOCKS = 16
CANDS = 24
PAIR = 2 * TILE
COLS = 256
LOW = -3.0e38
MESH = pl.DeviceIdType.MESH
BF16 = jnp.bfloat16
F32 = jnp.float32
I32 = jnp.int32


def remote(src, dst, send_sem, recv_sem, device):
    return pltpu.make_async_remote_copy(
        src_ref=src, dst_ref=dst, send_sem=send_sem, recv_sem=recv_sem, device_id=device, device_id_type=MESH
    )


def iota(shape, dim):
    return lax.broadcasted_iota(I32, shape, dim)


def to_column(row):
    n = row.shape[1]
    return jnp.sum(jnp.where(iota((n, n), 0) == iota((n, n), 1), jnp.broadcast_to(row, (n, n)), 0), axis=1, keepdims=True)


def to_row(col):
    n = col.shape[0]
    return jnp.sum(jnp.where(iota((n, n), 0) == iota((n, n), 1), jnp.broadcast_to(col, (n, n)), 0), axis=0, keepdims=True)


def gray(k):
    return k + (k // 2) * (1 - 2 * (k % 2))


def pair_of(n):
    s = jnp.where(n >= 1, 1, 0) + jnp.where(n >= 4, 1, 0) + jnp.where(n >= 9, 1, 0)
    m = n - s * s
    odd = m % 2
    return gray(s + odd * (m // 2 - s)), gray(m // 2 + odd * (s - m // 2))


def kernel(
    des, proto, cand, pos, loss_o, dg_o, pg_o,
    tab0, tab1, tab2, tab3, rr0, rr1, rr2, rr3,
    send, arr_m, arr_o, des_m, des_o, dt_m, dt_o, grads, stage, merge, from_up, from_down, from_y, far_y, runs, core_in, dg_s,
    prow, m_run, s_run, pick, total, req_v, req_in, order_v, req_own, req_s, order_s,
    ld_sem, des_sem, out_sem, loc_sem, own_sem, rq_s, rq_r, ag_s, ag_r, rl_s, rl_r, gy_s, gy_r, ha_s, ha_r, f_s, fm_r, fo_r, b_s, b_r,
    fy_s, fy_r, mg_s, mg_r, rs_s, rs_r, y_s, y_r, c_s, c_r,
):
    p, d = lax.axis_index("proto"), lax.axis_index("design")
    x, z, y, r = p // SIDE, p % SIDE, d // 2, d % 2
    tab, rr = (tab0, tab1, tab2, tab3), (rr0, rr1, rr2, rr3)

    def owner(ku, kv):
        return ((x + ku * (1 - r) + kv * r) % SIDE) * SIDE + (z + ku * r + kv * (1 - r)) % SIDE

    def along_u(k, core):
        return (owner(k, 0), y * 2 + core)

    def along_v(k, core):
        return (owner(0, k), y * 2 + core)

    def along_y(k):
        return (p, ((y + k) % SIDE) * 2 + r)

    def group(k):
        return pl.ds(((y + k) % SIDE) * 4, 4)

    sibling = (p, y * 2 + 1 - r)
    my_cols = pl.ds(pl.multiple_of(r * HALF, HALF), HALF)
    other_cols = pl.ds(pl.multiple_of((1 - r) * HALF, HALF), HALF)

    turns = (0, 1, 3, 2)

    def load(j):
        rows = pl.ds(pl.multiple_of(((y + turns[j]) % SIDE) * HALF, HALF), HALF)
        return pltpu.make_async_copy(proto.at[rows, my_cols], stage.at[j % 2], ld_sem.at[j])

    load(0).start()
    load(1).start()
    designs_in = [
        pltpu.make_async_copy(des.at[:, my_cols], des_m, des_sem.at[0]),
        pltpu.make_async_copy(des.at[:, other_cols], des_o, des_sem.at[1]),
    ]
    for c in designs_in:
        c.start()

    barrier = pltpu.get_barrier_semaphore()
    partners = [sibling]
    for k in (1, 2, 3):
        partners += [along_v(k, r), along_v(k, 1 - r), along_u(k, 1 - r), along_y(k)]
    partners += [along_u(1, r), along_u(3, r)]
    for q in partners:
        pl.semaphore_signal(barrier, inc=1, device_id=q, device_id_type=MESH)

    row = cand[...]
    col = to_column(row)
    same = (row >> 4) == (col >> 4)
    rank = jnp.sum(jnp.where(same & (iota((CANDS, CANDS), 1) < iota((CANDS, CANDS), 0)), 1, 0), axis=1, keepdims=True)
    slot = (col >> 4) * 2 + rank
    hit = slot == iota((CANDS, TILE), 1)
    wanted = jnp.sum(jnp.where(hit, (col & 15) + 1, 0), axis=0, keepdims=True) - 1
    req_v[...] = jnp.broadcast_to(wanted, (8, TILE))
    block = pos[...] >> 7
    spot = jnp.sum(jnp.where(col == block, slot, 0), axis=0, keepdims=True)
    prow[...] = spot * TILE + (pos[...] & 127)
    pltpu.make_async_copy(req_v, req_own, own_sem).start()

    pl.semaphore_wait(barrier, len(partners))

    req_in[0] = req_v[...]
    requests = [remote(req_v, req_in.at[1], rq_s.at[0], rq_r.at[1], sibling)]
    for k in (1, 2, 3):
        back = (SIDE - k) * 2
        requests.append(remote(req_v, req_in.at[back], rq_s.at[2 * k - 1], rq_r.at[back], along_v(k, r)))
        requests.append(remote(req_v, req_in.at[back + 1], rq_s.at[2 * k], rq_r.at[back + 1], along_u(k, 1 - r)))
    for c in requests:
        c.start()

    def own_chunk(k, way):
        low, count = ((0, 4), (2, 2), (0, 4), (0, 2))[k]
        part = pl.ds(((y + k) % SIDE) * 4 + low, count)
        dst = tab3 if way == 0 else tab1
        return remote(tab0.at[part], dst.at[part], ag_s.at[way, k], ag_r.at[way, k], along_u(1 if way == 0 else 3, r))

    for j in range(4):
        load(j).wait()
        for b in range(4):
            tab0[((y + turns[j]) % SIDE) * 4 + b] = stage[j % 2, TILE * b : TILE * (b + 1)].astype(BF16)
        if j < 2:
            own_chunk(turns[j], 0).start()
            own_chunk(turns[j], 1).start()
            load(j + 2).start()

    for c in designs_in:
        c.wait()

    @pl.loop(0, 4)
    def _(i):
        part = pl.ds(pl.multiple_of(i * COLS, COLS), COLS)
        dt_m[:, part] = des_m[part, :].T
        dt_o[:, part] = des_o[part, :].T

    for n in range(1, 8):
        remote(req_v, req_in.at[n], rq_s.at[0], rq_r.at[n], sibling).wait_recv()
    to_scalars = pltpu.make_async_copy(req_in, req_s, loc_sem.at[0])
    to_scalars.start()
    to_scalars.wait()

    def wanted_blocks(ku):
        first = owner(ku, 0) * 2
        for n in (0, 2, 3, 6, 7, 1, 4, 5):
            for i in range(2):
                val = tab[ku][jnp.maximum(req_s[n, 0, first + i], 0)]
                if n == 0:
                    arr_m[0, ku, i] = val
                else:
                    send[n, ku, i] = val
            if n:
                fetched(n, ku).start()

    def fetched(n, ku):
        k, so = n // 2, n % 2
        back = (SIDE - k) % SIDE
        if so == 0:
            return remote(send.at[n, ku], arr_m.at[back, ku], f_s.at[n, ku], fm_r.at[back, ku], along_v(k, r))
        return remote(send.at[n, ku], arr_o.at[back, ku], f_s.at[n, ku], fo_r.at[back, ku], along_v(k, 1 - r))

    def relay(way):
        part = pl.ds(4 * y + 2 * way, 2)
        src, to = (tab3, 1) if way == 0 else (tab1, 3)
        return remote(src.at[part], tab2.at[part], rl_s.at[way], rl_r.at[way], along_u(to, r))

    def share(k):
        return remote(tab2.at[group(0)], tab2.at[group(0)], gy_s.at[k], gy_r.at[SIDE - k], along_y(k))

    def hand(way, k):
        part = pl.ds(4 * y + (2 if k == 1 else 0), 2)
        src = tab3 if way == 0 else tab1
        return remote(src.at[part], src.at[part], ha_s.at[way, k // 2], ha_r.at[way, k // 2], along_y(k))

    for way in (0, 1):
        own_chunk(0, way).wait_recv()
        relay(way).start()
        hand(way, 1).start()
        hand(way, 3).start()
    for k in (3, 2):
        own_chunk(k, 0).start()
        own_chunk(k, 1).start()
    for way in (0, 1):
        relay(way).wait_recv()
    for k in (1, 3, 2):
        share(k).start()
    wanted_blocks(0)
    for way, ku in ((1, 1), (0, 3)):
        for k in (1, 2, 3):
            own_chunk(k, way).wait_recv()
        hand(way, 1).wait_recv()
        hand(way, 3).wait_recv()
        wanted_blocks(ku)
    for k in (1, 2, 3):
        remote(tab2.at[group(0)], tab2.at[group(0)], gy_s.at[k], gy_r.at[k], sibling).wait_recv()
    wanted_blocks(2)

    for ku in range(4):
        first = owner(ku, 0) * 2
        eye = iota((8, TILE), 1)
        reqs = req_in[:, 0, :]
        ids = [jnp.sum(jnp.where(eye == first + i, reqs, 0), axis=1, keepdims=True) for i in range(2)]
        ids = jnp.concatenate(ids, axis=0)
        place = iota((BLOCKS, 1), 0)
        entry = (place % 8) * 2 + place // 8
        key = ids * BLOCKS + entry
        rank = jnp.sum(jnp.where(to_row(key) < key, 1, 0), axis=1, keepdims=True)
        at = rank == iota((BLOCKS, TILE), 1)
        follows = jnp.sum(jnp.where((to_row(key) < key) & (to_row(ids) == ids), 1, 0), axis=1, keepdims=True)
        lane = iota((BLOCKS, TILE), 1)
        rows = [
            jnp.sum(jnp.where(at, entry, 0), axis=0, keepdims=True),
            jnp.sum(jnp.where(at & (follows == 0), 1, 0), axis=0, keepdims=True),
            jnp.maximum(jnp.sum(jnp.where(ids <= lane, 1, 0), axis=0, keepdims=True) - 1, 0),
            jnp.sum(jnp.where(ids == lane, 1, 0), axis=0, keepdims=True),
        ]
        for i in range(4):
            order_v[ku, i : i + 1, :] = rows[i]
    order_copy = pltpu.make_async_copy(order_v, order_s, loc_sem.at[1])
    order_copy.start()
    pltpu.make_async_copy(req_v, req_own, own_sem).wait()

    def logits_of(ku, kv, part):
        o = owner(ku, kv)
        left = jnp.dot(arr_m[kv, ku].reshape(PAIR, HALF), dt_m[:, part], preferred_element_type=F32)
        right = jnp.dot(arr_o[ku, kv].reshape(PAIR, HALF), dt_o[:, part], preferred_element_type=F32)
        rows = iota((PAIR, COLS), 0)
        held = jnp.where(rows < TILE, req_own[0, o * 2], req_own[0, o * 2 + 1]) >= 0
        target = rows + o * PAIR == prow[:, part]
        return jnp.where(held, (left + right) * D**-0.5, LOW), target

    m_run[...] = jnp.full((1, ROWS), LOW, F32)
    s_run[...] = jnp.zeros((1, ROWS), F32)
    pick[...] = jnp.zeros((1, ROWS), F32)

    @pl.loop(0, 16)
    def _(n):
        ku, kv = pair_of(n)

        @pl.when(kv != 0)
        def _():
            remote(send.at[1, 0], arr_m.at[kv, ku], f_s.at[1, 0], fm_r.at[kv, ku], sibling).wait_recv()

        remote(send.at[1, 0], arr_o.at[ku, kv], f_s.at[1, 0], fo_r.at[ku, kv], sibling).wait_recv()

        @pl.loop(0, ROWS // COLS)
        def _(i):
            part = pl.ds(pl.multiple_of(i * COLS, COLS), COLS)
            logits, target = logits_of(ku, kv, part)
            pick[:, part] += jnp.sum(jnp.where(target, logits, 0.0), axis=0, keepdims=True)
            before = m_run[:, part]
            now = jnp.maximum(before, jnp.max(logits, axis=0, keepdims=True))
            m_run[:, part] = now
            s_run[:, part] = s_run[:, part] * jnp.exp(before - now) + jnp.sum(jnp.exp(logits - now), axis=0, keepdims=True)

    total[...] = m_run[...] + jnp.log(s_run[...])
    loss_o[...] = total[...] - pick[...]

    for n in range(1, 8):
        for ku in range(4):
            fetched(n, ku).wait_send()
    for c in requests:
        c.wait_send()
    for k in range(4):
        own_chunk(k, 0).wait_send()
        own_chunk(k, 1).wait_send()
    for way in (0, 1):
        relay(way).wait_send()
        hand(way, 1).wait_send()
        hand(way, 3).wait_send()
    for k in (1, 2, 3):
        share(k).wait_send()

    def back_mine(ku, kv, k):
        back = (SIDE - kv) % SIDE
        return remote(send.at[kv * 2, ku], rr[k].at[pl.ds(back * 4, 2)], b_s.at[kv * 2, ku], b_r.at[k, back, 0], along_v(kv, r))

    def back_other(ku, kv, k):
        back = (SIDE - ku) % SIDE
        return remote(send.at[ku * 2 + 1, kv], rr[k].at[pl.ds(back * 4 + 2, 2)], b_s.at[ku * 2 + 1, kv], b_r.at[k, back, 1], along_u(ku, 1 - r))

    def second_pass(n):
        ku, kv = pair_of(15 - n)

        @pl.loop(0, ROWS // COLS)
        def _(i):
            part = pl.ds(pl.multiple_of(i * COLS, COLS), COLS)
            logits, target = logits_of(ku, kv, part)
            grads[kv, ku, :, part] = (jnp.exp(logits - total[:, part]) - jnp.where(target, 1.0, 0.0)).astype(BF16)

        mine = jnp.dot(grads[kv, ku], des_m[...], preferred_element_type=F32).astype(BF16).reshape(2, TILE, HALF)
        send[kv * 2, ku] = mine
        other = jnp.dot(grads[kv, ku], des_o[...], preferred_element_type=F32).astype(BF16).reshape(2, TILE, HALF)
        send[ku * 2 + 1, kv] = other
        for k in range(4):

            @pl.when(ku == k)
            def _():
                @pl.when(kv == 0)
                def _():
                    rr[k][0:2] = send[0, k]

                @pl.when(kv != 0)
                def _():
                    back_mine(ku, kv, k).start()

            @pl.when(kv == k)
            def _():
                back_other(ku, kv, k).start()

    def sums(ku):
        for n in range(1, 8):
            k, so = n // 2, n % 2
            remote(send.at[1, 0], rr[ku].at[pl.ds(2 * n, 2)], b_s.at[1, 0], b_r.at[ku, k, so], sibling).wait_recv()

        @pl.loop(0, TILE // 16)
        def _(i):
            part = pl.ds(pl.multiple_of(i * 16, 16), 16)
            acc = jnp.zeros((16, HALF), F32)
            for t in range(BLOCKS):
                val = rr[ku][order_s[ku, 0, t], part, :].astype(F32)
                acc = jnp.where(order_s[ku, 1, t] == 1, val, acc + val)
                runs[t] = acc
            for j in range(BLOCKS):
                val = runs[order_s[ku, 2, j]]
                tab[ku][j, part, :] = jnp.where(order_s[ku, 3, j] > 0, val, 0.0).astype(BF16)

    def design_grad(q, h):
        part = pl.ds(q * COLS, COLS)
        acc = stage.at[0, pl.ds(0, COLS)]
        acc[...] = jnp.zeros((COLS, HALF), F32)

        @pl.loop(0, 4)
        def _(k):
            lhs = grads[k, :, :, part] if h == 0 else grads[:, k, :, part]
            rhs = arr_m[k] if h == 0 else arr_o[k]
            acc[...] += lax.dot_general(
                lhs.reshape(ROWS, COLS), rhs.reshape(ROWS, HALF), (((0,), (0,)), ((), ())), preferred_element_type=F32
            )

        dg_s[q, h] = acc[...].astype(BF16)
        dg_out(q, h).start()

    def dg_out(q, h):
        cols = my_cols if h == 0 else other_cols
        return pltpu.make_async_copy(dg_s.at[q, h], dg_o.at[pl.ds(q * COLS, COLS), cols], out_sem.at[q, h])

    def far_along_y(k):
        return remote(tab2.at[group(k)], far_y.at[SIDE - k], fy_s.at[k], fy_r.at[SIDE - k], along_y(k))

    def far(way):
        part = pl.ds(4 * y + 2 * way, 2)
        return remote(tab2.at[part], merge.at[way], mg_s.at[way], mg_r.at[way], along_u(1 if way == 0 else 3, r))

    def near(k, way):
        if way == 0:
            return remote(tab1.at[group(k)], from_down.at[k], rs_s.at[0, k], rs_r.at[0, k], along_u(1, r))
        return remote(tab3.at[group(k)], from_up.at[k], rs_s.at[1, k], rs_r.at[1, k], along_u(3, r))

    def to_y(k):
        return remote(tab0.at[group(k)], from_y.at[SIDE - k], y_s.at[k], y_r.at[SIDE - k], along_y(k))

    pl.loop(0, 12)(second_pass)
    order_copy.wait()
    sums(2)
    for k in (1, 3, 2):
        far_along_y(k).start()
    pl.loop(12, 16)(second_pass)
    design_grad(0, 0)
    design_grad(0, 1)
    sums(3)
    near(1, 1).start()
    near(3, 1).start()
    design_grad(1, 0)
    sums(1)
    near(1, 0).start()
    near(3, 0).start()
    sums(0)
    for k in (1, 3, 2):
        remote(tab2.at[group(0)], far_y.at[k], fy_s.at[k], fy_r.at[k], sibling).wait_recv()
    for b in range(4):
        val = tab2[4 * y + b].astype(F32)
        for k in (1, 2, 3):
            val += far_y[k, b].astype(F32)
        tab2[4 * y + b] = val.astype(BF16)
    far(0).start()
    far(1).start()
    near(2, 0).start()
    near(2, 1).start()
    design_grad(1, 1)

    def add_near(k):
        near(k, 0).wait_recv()
        near(k, 1).wait_recv()
        for b in range(4):
            at = ((y + k) % SIDE) * 4 + b
            val = tab0[at].astype(F32) + from_up[k, b].astype(F32) + from_down[k, b].astype(F32)
            tab0[at] = val.astype(BF16)

    add_near(1)
    to_y(1).start()
    add_near(3)
    to_y(3).start()
    for way in (0, 1):
        src = tab1 if way == 0 else tab3
        far(way).wait_recv()
        for b in range(2):
            at = 4 * y + 2 * way + b
            src[at] = (src[at].astype(F32) + merge[way, b].astype(F32)).astype(BF16)
        near(0, way).start()
    design_grad(2, 0)
    add_near(2)
    to_y(2).start()
    design_grad(2, 1)
    design_grad(3, 0)
    design_grad(3, 1)
    add_near(0)
    for k in (1, 3, 2):
        remote(tab0.at[pl.ds(0, 4)], from_y.at[k], y_s.at[0], y_r.at[k], sibling).wait_recv()

    def reduced(b):
        val = tab0[4 * y + b].astype(F32)
        for k in (1, 2, 3):
            val += from_y[k, b].astype(F32)
        return val

    for i in range(2):
        stage[1, pl.ds(PAIR + i * TILE, TILE)] = reduced(2 * (1 - r) + i)
    cross = remote(stage.at[1, pl.ds(PAIR, PAIR)], core_in, c_s, c_r, sibling)
    cross.start()
    for i in range(2):
        stage[1, pl.ds(i * TILE, TILE)] = reduced(2 * r + i)
    outs = [pltpu.make_async_copy(stage.at[1, pl.ds(0, PAIR)], pg_o.at[:, my_cols], loc_sem.at[2])]
    outs[0].start()
    cross.wait_recv()
    outs.append(pltpu.make_async_copy(core_in, pg_o.at[:, other_cols], loc_sem.at[3]))
    outs[1].start()

    for kv in range(4):
        for ku in range(4):
            if kv:
                back_mine(ku, kv, ku).wait_send()
            back_other(ku, kv, kv).wait_send()
    for k in range(4):
        near(k, 0).wait_send()
        near(k, 1).wait_send()
        if k:
            far_along_y(k).wait_send()
            to_y(k).wait_send()
        for h in range(2):
            dg_out(k, h).wait()
    far(0).wait_send()
    far(1).wait_send()
    cross.wait_send()
    for c in outs:
        c.wait()


def settle(losses, design_grad, proto_grad, losses_o, design_grad_o, proto_grad_o, one, many, few, sems):
    moves = [(losses, one, losses_o)]
    for i in range(4):
        part = pl.ds(i * COLS, COLS)
        moves.append((design_grad.at[part], many.at[part], design_grad_o.at[part]))
    for i in range(2):
        part = pl.ds(i * TILE, TILE)
        moves.append((proto_grad.at[part], few.at[part], proto_grad_o.at[part]))
    reads = [pltpu.make_async_copy(a, b, sems.at[0, n]) for n, (a, b, c) in enumerate(moves)]
    writes = [pltpu.make_async_copy(b, c, sems.at[1, n]) for n, (a, b, c) in enumerate(moves)]
    for c in reads:
        c.start()
    for a, b in zip(reads, writes):
        a.wait()
        b.start()
    for c in writes:
        c.wait()


def body(designs, prototypes, candidates, positives):
    vmem = lambda shape, dtype: pltpu.VMEM(shape, dtype)
    dma = lambda *shape: pltpu.SemaphoreType.DMA(shape)
    blocks = (BLOCKS, TILE, HALF)
    pairs = (SIDE, SIDE, 2, TILE, HALF)
    losses, design_grad, proto_grad = pl.pallas_call(
        kernel,
        out_shape=(
            jax.ShapeDtypeStruct((1, ROWS), F32),
            jax.ShapeDtypeStruct((ROWS, D), BF16),
            jax.ShapeDtypeStruct((PAIR, D), F32),
        ),
        in_specs=[
            pl.BlockSpec(memory_space=pl.ANY),
            pl.BlockSpec(memory_space=pl.ANY),
            pl.BlockSpec(memory_space=pltpu.VMEM),
            pl.BlockSpec(memory_space=pltpu.VMEM),
        ],
        out_specs=(
            pl.BlockSpec(memory_space=pltpu.VMEM),
            pl.BlockSpec(memory_space=pl.ANY),
            pl.BlockSpec(memory_space=pl.ANY),
        ),
        scratch_shapes=[
            *[vmem(blocks, BF16) for _ in range(8)],
            vmem((8, SIDE, 2, TILE, HALF), BF16),
            vmem(pairs, BF16),
            vmem(pairs, BF16),
            vmem((ROWS, HALF), BF16),
            vmem((ROWS, HALF), BF16),
            vmem((HALF, ROWS), BF16),
            vmem((HALF, ROWS), BF16),
            vmem((SIDE, SIDE, PAIR, ROWS), BF16),
            vmem((2, HALF, HALF), F32),
            vmem((2, 2, TILE, HALF), BF16),
            vmem((4, 4, TILE, HALF), BF16),
            vmem((4, 4, TILE, HALF), BF16),
            vmem((4, 4, TILE, HALF), BF16),
            vmem((4, 4, TILE, HALF), BF16),
            vmem((BLOCKS, 16, HALF), F32),
            vmem((PAIR, HALF), F32),
            vmem((4, 2, COLS, HALF), BF16),
            vmem((1, ROWS), I32),
            *[vmem((1, ROWS), F32) for _ in range(4)],
            vmem((8, TILE), I32),
            vmem((8, 8, TILE), I32),
            vmem((4, 8, TILE), I32),
            pltpu.SMEM((8, TILE), I32),
            pltpu.SMEM((8, 8, TILE), I32),
            pltpu.SMEM((4, 8, TILE), I32),
            dma(4),
            dma(2),
            dma(4, 2),
            dma(4),
            pltpu.SemaphoreType.DMA,
            dma(8),
            dma(8),
            dma(2, 4),
            dma(2, 4),
            dma(2),
            dma(2),
            dma(4),
            dma(4),
            dma(2, 2),
            dma(2, 2),
            dma(8, 4),
            dma(4, 4),
            dma(4, 4),
            dma(8, 4),
            dma(4, 4, 2),
            dma(4),
            dma(4),
            dma(2),
            dma(2),
            dma(2, 4),
            dma(2, 4),
            dma(4),
            dma(4),
            pltpu.SemaphoreType.DMA,
            pltpu.SemaphoreType.DMA,
        ],
        compiler_params=pltpu.CompilerParams(
            collective_id=0, has_side_effects=True, vmem_limit_bytes=62 * 2**20
        ),
    )(designs, prototypes, candidates, positives.reshape(1, ROWS))
    losses, design_grad, proto_grad = pl.pallas_call(
        settle,
        out_shape=(
            jax.ShapeDtypeStruct((1, ROWS), F32),
            jax.ShapeDtypeStruct((ROWS, D), BF16),
            jax.ShapeDtypeStruct((PAIR, D), F32),
        ),
        in_specs=[pl.BlockSpec(memory_space=pl.ANY)] * 3,
        out_specs=(pl.BlockSpec(memory_space=pl.ANY),) * 3,
        scratch_shapes=[vmem((1, ROWS), F32), vmem((ROWS, D), BF16), vmem((PAIR, D), F32), dma(2, 7)],
    )(losses, design_grad, proto_grad)
    return losses.reshape(ROWS), design_grad, proto_grad


def solution(mesh):
    return jax.shard_map(
        body,
        mesh=mesh,
        in_specs=(
            P(("proto", "design"), None),
            P("proto", None),
            P(("proto", "design"), None),
            P(("proto", "design")),
        ),
        out_specs=(
            P(("proto", "design")),
            P(("proto", "design"), None),
            P(("proto", "design"), None),
        ),
        check_vma=False,
    )
```

```python
import jax
import jax.numpy as jnp
from jax import lax
from jax.experimental import pallas as pl
from jax.experimental.pallas import tpu as pltpu
from jax.sharding import PartitionSpec as P

D = 1024
HALF = 512
TILE = 128
ROWS = 1024
SIDE = 4
BLOCKS = 16
CANDS = 24
PAIR = 2 * TILE
COLS = 256
LOW = -3.0e38
MESH = pl.DeviceIdType.MESH
BF16 = jnp.bfloat16
F32 = jnp.float32
I32 = jnp.int32


def remote(src, dst, send_sem, recv_sem, device):
    return pltpu.make_async_remote_copy(
        src_ref=src, dst_ref=dst, send_sem=send_sem, recv_sem=recv_sem, device_id=device, device_id_type=MESH
    )


def iota(shape, dim):
    return lax.broadcasted_iota(I32, shape, dim)


def to_column(row):
    n = row.shape[1]
    return jnp.sum(jnp.where(iota((n, n), 0) == iota((n, n), 1), jnp.broadcast_to(row, (n, n)), 0), axis=1, keepdims=True)


def to_row(col):
    n = col.shape[0]
    return jnp.sum(jnp.where(iota((n, n), 0) == iota((n, n), 1), jnp.broadcast_to(col, (n, n)), 0), axis=0, keepdims=True)


def gray(k):
    return k + (k // 2) * (1 - 2 * (k % 2))


def pair_of(n):
    s = jnp.where(n >= 1, 1, 0) + jnp.where(n >= 4, 1, 0) + jnp.where(n >= 9, 1, 0)
    m = n - s * s
    odd = m % 2
    return gray(s + odd * (m // 2 - s)), gray(m // 2 + odd * (s - m // 2))


def kernel(
    des, proto, cand, pos, loss_o, dg_o, pg_o,
    tab0, tab1, tab2, tab3, rr0, rr1, rr2, rr3,
    send, arr_m, arr_o, des_m, des_o, dt_m, dt_o, grads, stage, merge, from_up, from_down, from_y, far_y, runs, core_in, dg_s,
    prow, m_run, s_run, pick, total, req_v, req_in, order_v, req_own, req_s, order_s,
    ld_sem, des_sem, out_sem, loc_sem, own_sem, rq_s, rq_r, ag_s, ag_r, rl_s, rl_r, gy_s, gy_r, ha_s, ha_r, f_s, fm_r, fo_r, b_s, b_r,
    fy_s, fy_r, mg_s, mg_r, rs_s, rs_r, y_s, y_r, c_s, c_r,
):
    p, d = lax.axis_index("proto"), lax.axis_index("design")
    x, z, y, r = p // SIDE, p % SIDE, d // 2, d % 2
    tab, rr = (tab0, tab1, tab2, tab3), (rr0, rr1, rr2, rr3)

    def owner(ku, kv):
        return ((x + ku * (1 - r) + kv * r) % SIDE) * SIDE + (z + ku * r + kv * (1 - r)) % SIDE

    def along_u(k, core):
        return (owner(k, 0), y * 2 + core)

    def along_v(k, core):
        return (owner(0, k), y * 2 + core)

    def along_y(k):
        return (p, ((y + k) % SIDE) * 2 + r)

    def group(k):
        return pl.ds(((y + k) % SIDE) * 4, 4)

    sibling = (p, y * 2 + 1 - r)
    my_cols = pl.ds(pl.multiple_of(r * HALF, HALF), HALF)
    other_cols = pl.ds(pl.multiple_of((1 - r) * HALF, HALF), HALF)

    turns = (0, 1, 3, 2)

    def load(j):
        rows = pl.ds(pl.multiple_of(((y + turns[j]) % SIDE) * HALF, HALF), HALF)
        return pltpu.make_async_copy(proto.at[rows, my_cols], stage.at[j % 2], ld_sem.at[j])

    load(0).start()
    load(1).start()
    designs_in = [
        pltpu.make_async_copy(des.at[:, my_cols], des_m, des_sem.at[0]),
        pltpu.make_async_copy(des.at[:, other_cols], des_o, des_sem.at[1]),
    ]
    for c in designs_in:
        c.start()

    barrier = pltpu.get_barrier_semaphore()
    partners = [sibling]
    for k in (1, 2, 3):
        partners += [along_v(k, r), along_v(k, 1 - r), along_u(k, 1 - r), along_y(k)]
    partners += [along_u(1, r), along_u(3, r)]
    for q in partners:
        pl.semaphore_signal(barrier, inc=1, device_id=q, device_id_type=MESH)

    row = cand[...]
    col = to_column(row)
    same = (row >> 4) == (col >> 4)
    rank = jnp.sum(jnp.where(same & (iota((CANDS, CANDS), 1) < iota((CANDS, CANDS), 0)), 1, 0), axis=1, keepdims=True)
    slot = (col >> 4) * 2 + rank
    hit = slot == iota((CANDS, TILE), 1)
    wanted = jnp.sum(jnp.where(hit, (col & 15) + 1, 0), axis=0, keepdims=True) - 1
    req_v[...] = jnp.broadcast_to(wanted, (8, TILE))
    block = pos[...] >> 7
    spot = jnp.sum(jnp.where(col == block, slot, 0), axis=0, keepdims=True)
    prow[...] = spot * TILE + (pos[...] & 127)
    pltpu.make_async_copy(req_v, req_own, own_sem).start()

    pl.semaphore_wait(barrier, len(partners))

    req_in[0] = req_v[...]
    requests = [remote(req_v, req_in.at[1], rq_s.at[0], rq_r.at[1], sibling)]
    for k in (1, 2, 3):
        back = (SIDE - k) * 2
        requests.append(remote(req_v, req_in.at[back], rq_s.at[2 * k - 1], rq_r.at[back], along_v(k, r)))
        requests.append(remote(req_v, req_in.at[back + 1], rq_s.at[2 * k], rq_r.at[back + 1], along_u(k, 1 - r)))
    for c in requests:
        c.start()

    def own_chunk(k, way):
        low, count = ((0, 4), (2, 2), (0, 4), (0, 2))[k]
        part = pl.ds(((y + k) % SIDE) * 4 + low, count)
        dst = tab3 if way == 0 else tab1
        return remote(tab0.at[part], dst.at[part], ag_s.at[way, k], ag_r.at[way, k], along_u(1 if way == 0 else 3, r))

    for j in range(4):
        load(j).wait()
        for b in range(4):
            tab0[((y + turns[j]) % SIDE) * 4 + b] = stage[j % 2, TILE * b : TILE * (b + 1)].astype(BF16)
        if j < 2:
            own_chunk(turns[j], 0).start()
            own_chunk(turns[j], 1).start()
            load(j + 2).start()

    for c in designs_in:
        c.wait()

    @pl.loop(0, 4)
    def _(i):
        part = pl.ds(pl.multiple_of(i * COLS, COLS), COLS)
        dt_m[:, part] = des_m[part, :].T
        dt_o[:, part] = des_o[part, :].T

    for n in range(1, 8):
        remote(req_v, req_in.at[n], rq_s.at[0], rq_r.at[n], sibling).wait_recv()
    to_scalars = pltpu.make_async_copy(req_in, req_s, loc_sem.at[0])
    to_scalars.start()
    to_scalars.wait()

    def wanted_blocks(ku):
        first = owner(ku, 0) * 2
        for n in (0, 2, 3, 6, 7, 1, 4, 5):
            for i in range(2):
                val = tab[ku][jnp.maximum(req_s[n, 0, first + i], 0)]
                if n == 0:
                    arr_m[0, ku, i] = val
                else:
                    send[n, ku, i] = val
            if n:
                fetched(n, ku).start()

    def fetched(n, ku):
        k, so = n // 2, n % 2
        back = (SIDE - k) % SIDE
        if so == 0:
            return remote(send.at[n, ku], arr_m.at[back, ku], f_s.at[n, ku], fm_r.at[back, ku], along_v(k, r))
        return remote(send.at[n, ku], arr_o.at[back, ku], f_s.at[n, ku], fo_r.at[back, ku], along_v(k, 1 - r))

    def relay(way):
        part = pl.ds(4 * y + 2 * way, 2)
        src, to = (tab3, 1) if way == 0 else (tab1, 3)
        return remote(src.at[part], tab2.at[part], rl_s.at[way], rl_r.at[way], along_u(to, r))

    def share(k):
        return remote(tab2.at[group(0)], tab2.at[group(0)], gy_s.at[k], gy_r.at[SIDE - k], along_y(k))

    def hand(way, k):
        part = pl.ds(4 * y + (2 if k == 1 else 0), 2)
        src = tab3 if way == 0 else tab1
        return remote(src.at[part], src.at[part], ha_s.at[way, k // 2], ha_r.at[way, k // 2], along_y(k))

    for way in (0, 1):
        own_chunk(0, way).wait_recv()
        relay(way).start()
        hand(way, 1).start()
        hand(way, 3).start()
    for k in (3, 2):
        own_chunk(k, 0).start()
        own_chunk(k, 1).start()
    for way in (0, 1):
        relay(way).wait_recv()
    for k in (1, 3, 2):
        share(k).start()
    wanted_blocks(0)
    for way, ku in ((1, 1), (0, 3)):
        for k in (1, 2, 3):
            own_chunk(k, way).wait_recv()
        hand(way, 1).wait_recv()
        hand(way, 3).wait_recv()
        wanted_blocks(ku)
    for k in (1, 2, 3):
        remote(tab2.at[group(0)], tab2.at[group(0)], gy_s.at[k], gy_r.at[k], sibling).wait_recv()
    wanted_blocks(2)

    for ku in range(4):
        first = owner(ku, 0) * 2
        eye = iota((8, TILE), 1)
        reqs = req_in[:, 0, :]
        ids = [jnp.sum(jnp.where(eye == first + i, reqs, 0), axis=1, keepdims=True) for i in range(2)]
        ids = jnp.concatenate(ids, axis=0)
        place = iota((BLOCKS, 1), 0)
        entry = (place % 8) * 2 + place // 8
        key = ids * BLOCKS + entry
        rank = jnp.sum(jnp.where(to_row(key) < key, 1, 0), axis=1, keepdims=True)
        at = rank == iota((BLOCKS, TILE), 1)
        follows = jnp.sum(jnp.where((to_row(key) < key) & (to_row(ids) == ids), 1, 0), axis=1, keepdims=True)
        lane = iota((BLOCKS, TILE), 1)
        rows = [
            jnp.sum(jnp.where(at, entry, 0), axis=0, keepdims=True),
            jnp.sum(jnp.where(at & (follows == 0), 1, 0), axis=0, keepdims=True),
            jnp.maximum(jnp.sum(jnp.where(ids <= lane, 1, 0), axis=0, keepdims=True) - 1, 0),
            jnp.sum(jnp.where(ids == lane, 1, 0), axis=0, keepdims=True),
        ]
        for i in range(4):
            order_v[ku, i : i + 1, :] = rows[i]
    order_copy = pltpu.make_async_copy(order_v, order_s, loc_sem.at[1])
    order_copy.start()
    pltpu.make_async_copy(req_v, req_own, own_sem).wait()

    def logits_of(ku, kv, part):
        o = owner(ku, kv)
        left = jnp.dot(arr_m[kv, ku].reshape(PAIR, HALF), dt_m[:, part], preferred_element_type=F32)
        right = jnp.dot(arr_o[ku, kv].reshape(PAIR, HALF), dt_o[:, part], preferred_element_type=F32)
        rows = iota((PAIR, COLS), 0)
        held = jnp.where(rows < TILE, req_own[0, o * 2], req_own[0, o * 2 + 1]) >= 0
        target = rows + o * PAIR == prow[:, part]
        return jnp.where(held, (left + right) * D**-0.5, LOW), target

    m_run[...] = jnp.full((1, ROWS), LOW, F32)
    s_run[...] = jnp.zeros((1, ROWS), F32)
    pick[...] = jnp.zeros((1, ROWS), F32)

    @pl.loop(0, 16)
    def _(n):
        ku, kv = pair_of(n)

        @pl.when(kv != 0)
        def _():
            remote(send.at[1, 0], arr_m.at[kv, ku], f_s.at[1, 0], fm_r.at[kv, ku], sibling).wait_recv()

        remote(send.at[1, 0], arr_o.at[ku, kv], f_s.at[1, 0], fo_r.at[ku, kv], sibling).wait_recv()

        @pl.loop(0, ROWS // COLS)
        def _(i):
            part = pl.ds(pl.multiple_of(i * COLS, COLS), COLS)
            logits, target = logits_of(ku, kv, part)
            pick[:, part] += jnp.sum(jnp.where(target, logits, 0.0), axis=0, keepdims=True)
            before = m_run[:, part]
            now = jnp.maximum(before, jnp.max(logits, axis=0, keepdims=True))
            m_run[:, part] = now
            s_run[:, part] = s_run[:, part] * jnp.exp(before - now) + jnp.sum(jnp.exp(logits - now), axis=0, keepdims=True)

    total[...] = m_run[...] + jnp.log(s_run[...])
    loss_o[...] = total[...] - pick[...]

    for n in range(1, 8):
        for ku in range(4):
            fetched(n, ku).wait_send()
    for c in requests:
        c.wait_send()
    for k in range(4):
        own_chunk(k, 0).wait_send()
        own_chunk(k, 1).wait_send()
    for way in (0, 1):
        relay(way).wait_send()
        hand(way, 1).wait_send()
        hand(way, 3).wait_send()
    for k in (1, 2, 3):
        share(k).wait_send()

    def back_mine(ku, kv, k):
        back = (SIDE - kv) % SIDE
        return remote(send.at[kv * 2, ku], rr[k].at[pl.ds(back * 4, 2)], b_s.at[kv * 2, ku], b_r.at[k, back, 0], along_v(kv, r))

    def back_other(ku, kv, k):
        back = (SIDE - ku) % SIDE
        return remote(send.at[ku * 2 + 1, kv], rr[k].at[pl.ds(back * 4 + 2, 2)], b_s.at[ku * 2 + 1, kv], b_r.at[k, back, 1], along_u(ku, 1 - r))

    def second_pass(n):
        ku, kv = pair_of(15 - n)

        @pl.loop(0, ROWS // COLS)
        def _(i):
            part = pl.ds(pl.multiple_of(i * COLS, COLS), COLS)
            logits, target = logits_of(ku, kv, part)
            grads[kv, ku, :, part] = (jnp.exp(logits - total[:, part]) - jnp.where(target, 1.0, 0.0)).astype(BF16)

        mine = jnp.dot(grads[kv, ku], des_m[...], preferred_element_type=F32).astype(BF16).reshape(2, TILE, HALF)
        send[kv * 2, ku] = mine
        other = jnp.dot(grads[kv, ku], des_o[...], preferred_element_type=F32).astype(BF16).reshape(2, TILE, HALF)
        send[ku * 2 + 1, kv] = other

        @pl.when((ku == 0) & (kv == 0))
        def _():
            rr[0][0:2] = send[0, 0]

        for k in (1, 2, 3):

            @pl.when((ku == k) & (kv == 0))
            def _():
                rr[k][0:2] = send[0, k]

            @pl.when((ku == k) & (kv != 0))
            def _():
                back_mine(ku, kv, k).start()

            @pl.when(kv == k)
            def _():
                back_other(ku, kv, k).start()

    def sums(ku):
        for n in range(1, 8):
            k, so = n // 2, n % 2
            remote(send.at[1, 0], rr[ku].at[pl.ds(2 * n, 2)], b_s.at[1, 0], b_r.at[ku, k, so], sibling).wait_recv()

        @pl.loop(0, TILE // 16)
        def _(i):
            part = pl.ds(pl.multiple_of(i * 16, 16), 16)
            acc = jnp.zeros((16, HALF), F32)
            for t in range(BLOCKS):
                val = rr[ku][order_s[ku, 0, t], part, :].astype(F32)
                acc = jnp.where(order_s[ku, 1, t] == 1, val, acc + val)
                runs[t] = acc
            for j in range(BLOCKS):
                val = runs[order_s[ku, 2, j]]
                tab[ku][j, part, :] = jnp.where(order_s[ku, 3, j] > 0, val, 0.0).astype(BF16)

    def design_grad(q, h):
        part = pl.ds(q * COLS, COLS)
        acc = stage.at[0, pl.ds(0, COLS)]
        acc[...] = jnp.zeros((COLS, HALF), F32)

        @pl.loop(0, 4)
        def _(k):
            lhs = grads[k, :, :, part] if h == 0 else grads[:, k, :, part]
            rhs = arr_m[k] if h == 0 else arr_o[k]
            acc[...] += lax.dot_general(
                lhs.reshape(ROWS, COLS), rhs.reshape(ROWS, HALF), (((0,), (0,)), ((), ())), preferred_element_type=F32
            )

        dg_s[q, h] = acc[...].astype(BF16)
        dg_out(q, h).start()

    def dg_out(q, h):
        cols = my_cols if h == 0 else other_cols
        return pltpu.make_async_copy(dg_s.at[q, h], dg_o.at[pl.ds(q * COLS, COLS), cols], out_sem.at[q, h])

    def far_along_y(k):
        return remote(tab2.at[group(k)], far_y.at[SIDE - k], fy_s.at[k], fy_r.at[SIDE - k], along_y(k))

    def far(way):
        part = pl.ds(4 * y + 2 * way, 2)
        return remote(tab2.at[part], merge.at[way], mg_s.at[way], mg_r.at[way], along_u(1 if way == 0 else 3, r))

    def near(k, way):
        if way == 0:
            return remote(tab1.at[group(k)], from_down.at[k], rs_s.at[0, k], rs_r.at[0, k], along_u(1, r))
        return remote(tab3.at[group(k)], from_up.at[k], rs_s.at[1, k], rs_r.at[1, k], along_u(3, r))

    def to_y(k):
        return remote(tab0.at[group(k)], from_y.at[SIDE - k], y_s.at[k], y_r.at[SIDE - k], along_y(k))

    pl.loop(0, 12)(second_pass)
    order_copy.wait()
    sums(2)
    for k in (1, 3, 2):
        far_along_y(k).start()
    pl.loop(12, 16)(second_pass)
    for kv in (1, 3, 2):
        back_mine(0, kv, 0).start()
    design_grad(0, 0)
    sums(3)
    near(2, 1).start()
    sums(1)
    near(2, 0).start()
    for ku in (0, 1, 3, 2):
        back_other(ku, 0, 0).start()
    for k in (1, 3):
        near(k, 1).start()
        near(k, 0).start()
    design_grad(0, 1)
    design_grad(1, 0)
    for k in (1, 3, 2):
        remote(tab2.at[group(0)], far_y.at[k], fy_s.at[k], fy_r.at[k], sibling).wait_recv()
    for b in range(4):
        val = tab2[4 * y + b].astype(F32)
        for k in (1, 2, 3):
            val += far_y[k, b].astype(F32)
        tab2[4 * y + b] = val.astype(BF16)
    far(0).start()
    far(1).start()
    design_grad(1, 1)
    sums(0)

    def add_near(k):
        near(k, 0).wait_recv()
        near(k, 1).wait_recv()
        for b in range(4):
            at = ((y + k) % SIDE) * 4 + b
            val = tab0[at].astype(F32) + from_up[k, b].astype(F32) + from_down[k, b].astype(F32)
            tab0[at] = val.astype(BF16)

    add_near(2)
    to_y(2).start()
    design_grad(2, 0)
    add_near(1)
    to_y(1).start()
    design_grad(2, 1)
    add_near(3)
    to_y(3).start()
    for way in (0, 1):
        src = tab1 if way == 0 else tab3
        far(way).wait_recv()
        for b in range(2):
            at = 4 * y + 2 * way + b
            src[at] = (src[at].astype(F32) + merge[way, b].astype(F32)).astype(BF16)
        near(0, way).start()
    design_grad(3, 0)
    design_grad(3, 1)
    add_near(0)
    for k in (1, 3, 2):
        remote(tab0.at[pl.ds(0, 4)], from_y.at[k], y_s.at[0], y_r.at[k], sibling).wait_recv()

    def reduced(b):
        val = tab0[4 * y + b].astype(F32)
        for k in (1, 2, 3):
            val += from_y[k, b].astype(F32)
        return val

    for i in range(2):
        stage[1, pl.ds(PAIR + i * TILE, TILE)] = reduced(2 * (1 - r) + i)
    cross = remote(stage.at[1, pl.ds(PAIR, PAIR)], core_in, c_s, c_r, sibling)
    cross.start()
    for i in range(2):
        stage[1, pl.ds(i * TILE, TILE)] = reduced(2 * r + i)
    outs = [pltpu.make_async_copy(stage.at[1, pl.ds(0, PAIR)], pg_o.at[:, my_cols], loc_sem.at[2])]
    outs[0].start()
    cross.wait_recv()
    outs.append(pltpu.make_async_copy(core_in, pg_o.at[:, other_cols], loc_sem.at[3]))
    outs[1].start()

    for kv in range(4):
        for ku in range(4):
            if kv:
                back_mine(ku, kv, ku).wait_send()
            back_other(ku, kv, kv).wait_send()
    for k in range(4):
        near(k, 0).wait_send()
        near(k, 1).wait_send()
        if k:
            far_along_y(k).wait_send()
            to_y(k).wait_send()
        for h in range(2):
            dg_out(k, h).wait()
    far(0).wait_send()
    far(1).wait_send()
    cross.wait_send()
    for c in outs:
        c.wait()


def settle(losses, design_grad, proto_grad, losses_o, design_grad_o, proto_grad_o, one, many, few, sems):
    moves = [(losses, one, losses_o)]
    for i in range(4):
        part = pl.ds(i * COLS, COLS)
        moves.append((design_grad.at[part], many.at[part], design_grad_o.at[part]))
    for i in range(2):
        part = pl.ds(i * TILE, TILE)
        moves.append((proto_grad.at[part], few.at[part], proto_grad_o.at[part]))
    reads = [pltpu.make_async_copy(a, b, sems.at[0, n]) for n, (a, b, c) in enumerate(moves)]
    writes = [pltpu.make_async_copy(b, c, sems.at[1, n]) for n, (a, b, c) in enumerate(moves)]
    for c in reads:
        c.start()
    for a, b in zip(reads, writes):
        a.wait()
        b.start()
    for c in writes:
        c.wait()


def body(designs, prototypes, candidates, positives):
    vmem = lambda shape, dtype: pltpu.VMEM(shape, dtype)
    dma = lambda *shape: pltpu.SemaphoreType.DMA(shape)
    blocks = (BLOCKS, TILE, HALF)
    pairs = (SIDE, SIDE, 2, TILE, HALF)
    losses, design_grad, proto_grad = pl.pallas_call(
        kernel,
        out_shape=(
            jax.ShapeDtypeStruct((1, ROWS), F32),
            jax.ShapeDtypeStruct((ROWS, D), BF16),
            jax.ShapeDtypeStruct((PAIR, D), F32),
        ),
        in_specs=[
            pl.BlockSpec(memory_space=pl.ANY),
            pl.BlockSpec(memory_space=pl.ANY),
            pl.BlockSpec(memory_space=pltpu.VMEM),
            pl.BlockSpec(memory_space=pltpu.VMEM),
        ],
        out_specs=(
            pl.BlockSpec(memory_space=pltpu.VMEM),
            pl.BlockSpec(memory_space=pl.ANY),
            pl.BlockSpec(memory_space=pl.ANY),
        ),
        scratch_shapes=[
            *[vmem(blocks, BF16) for _ in range(8)],
            vmem((8, SIDE, 2, TILE, HALF), BF16),
            vmem(pairs, BF16),
            vmem(pairs, BF16),
            vmem((ROWS, HALF), BF16),
            vmem((ROWS, HALF), BF16),
            vmem((HALF, ROWS), BF16),
            vmem((HALF, ROWS), BF16),
            vmem((SIDE, SIDE, PAIR, ROWS), BF16),
            vmem((2, HALF, HALF), F32),
            vmem((2, 2, TILE, HALF), BF16),
            vmem((4, 4, TILE, HALF), BF16),
            vmem((4, 4, TILE, HALF), BF16),
            vmem((4, 4, TILE, HALF), BF16),
            vmem((4, 4, TILE, HALF), BF16),
            vmem((BLOCKS, 16, HALF), F32),
            vmem((PAIR, HALF), F32),
            vmem((4, 2, COLS, HALF), BF16),
            vmem((1, ROWS), I32),
            *[vmem((1, ROWS), F32) for _ in range(4)],
            vmem((8, TILE), I32),
            vmem((8, 8, TILE), I32),
            vmem((4, 8, TILE), I32),
            pltpu.SMEM((8, TILE), I32),
            pltpu.SMEM((8, 8, TILE), I32),
            pltpu.SMEM((4, 8, TILE), I32),
            dma(4),
            dma(2),
            dma(4, 2),
            dma(4),
            pltpu.SemaphoreType.DMA,
            dma(8),
            dma(8),
            dma(2, 4),
            dma(2, 4),
            dma(2),
            dma(2),
            dma(4),
            dma(4),
            dma(2, 2),
            dma(2, 2),
            dma(8, 4),
            dma(4, 4),
            dma(4, 4),
            dma(8, 4),
            dma(4, 4, 2),
            dma(4),
            dma(4),
            dma(2),
            dma(2),
            dma(2, 4),
            dma(2, 4),
            dma(4),
            dma(4),
            pltpu.SemaphoreType.DMA,
            pltpu.SemaphoreType.DMA,
        ],
        compiler_params=pltpu.CompilerParams(
            collective_id=0, has_side_effects=True, vmem_limit_bytes=62 * 2**20
        ),
    )(designs, prototypes, candidates, positives.reshape(1, ROWS))
    losses, design_grad, proto_grad = pl.pallas_call(
        settle,
        out_shape=(
            jax.ShapeDtypeStruct((1, ROWS), F32),
            jax.ShapeDtypeStruct((ROWS, D), BF16),
            jax.ShapeDtypeStruct((PAIR, D), F32),
        ),
        in_specs=[pl.BlockSpec(memory_space=pl.ANY)] * 3,
        out_specs=(pl.BlockSpec(memory_space=pl.ANY),) * 3,
        scratch_shapes=[vmem((1, ROWS), F32), vmem((ROWS, D), BF16), vmem((PAIR, D), F32), dma(2, 7)],
    )(losses, design_grad, proto_grad)
    return losses.reshape(ROWS), design_grad, proto_grad


def solution(mesh):
    return jax.shard_map(
        body,
        mesh=mesh,
        in_specs=(
            P(("proto", "design"), None),
            P("proto", None),
            P(("proto", "design"), None),
            P(("proto", "design")),
        ),
        out_specs=(
            P(("proto", "design")),
            P(("proto", "design"), None),
            P(("proto", "design"), None),
        ),
        check_vma=False,
    )
```

```python
import jax
import jax.numpy as jnp
from jax import lax
from jax.experimental import pallas as pl
from jax.experimental.pallas import tpu as pltpu
from jax.sharding import PartitionSpec as P

D = 1024
HALF = 512
TILE = 128
ROWS = 1024
SIDE = 4
BLOCKS = 16
CANDS = 24
PAIR = 2 * TILE
COLS = 256
LOW = -3.0e38
MESH = pl.DeviceIdType.MESH
BF16 = jnp.bfloat16
F32 = jnp.float32
I32 = jnp.int32


def remote(src, dst, send_sem, recv_sem, device):
    return pltpu.make_async_remote_copy(
        src_ref=src, dst_ref=dst, send_sem=send_sem, recv_sem=recv_sem, device_id=device, device_id_type=MESH
    )


def iota(shape, dim):
    return lax.broadcasted_iota(I32, shape, dim)


def to_column(row):
    n = row.shape[1]
    return jnp.sum(jnp.where(iota((n, n), 0) == iota((n, n), 1), jnp.broadcast_to(row, (n, n)), 0), axis=1, keepdims=True)


def to_row(col):
    n = col.shape[0]
    return jnp.sum(jnp.where(iota((n, n), 0) == iota((n, n), 1), jnp.broadcast_to(col, (n, n)), 0), axis=0, keepdims=True)


def gray(k):
    return k + (k // 2) * (1 - 2 * (k % 2))


def pair_of(n):
    s = jnp.where(n >= 1, 1, 0) + jnp.where(n >= 4, 1, 0) + jnp.where(n >= 9, 1, 0)
    m = n - s * s
    odd = m % 2
    return gray(s + odd * (m // 2 - s)), gray(m // 2 + odd * (s - m // 2))


def kernel(
    des, proto, cand, pos, loss_o, dg_o, pg_o,
    tab0, tab1, tab2, tab3, rr0, rr1, rr2, rr3,
    send, arr_m, arr_o, des_m, des_o, dt_m, dt_o, grads, stage, merge, from_up, from_down, from_y, far_y, runs, core_in, dg_s,
    prow, m_run, s_run, pick, total, req_v, req_in, order_v, req_own, req_s, order_s,
    ld_sem, des_sem, out_sem, loc_sem, own_sem, rq_s, rq_r, ag_s, ag_r, rl_s, rl_r, gy_s, gy_r, ha_s, ha_r, f_s, fm_r, fo_r, b_s, b_r,
    fy_s, fy_r, gv_s, gv_r, mg_s, mg_r, rs_s, rs_r, y_s, y_r, c_s, c_r,
):
    p, d = lax.axis_index("proto"), lax.axis_index("design")
    x, z, y, r = p // SIDE, p % SIDE, d // 2, d % 2
    tab, rr = (tab0, tab1, tab2, tab3), (rr0, rr1, rr2, rr3)

    def owner(ku, kv):
        return ((x + ku * (1 - r) + kv * r) % SIDE) * SIDE + (z + ku * r + kv * (1 - r)) % SIDE

    def along_u(k, core):
        return (owner(k, 0), y * 2 + core)

    def along_v(k, core):
        return (owner(0, k), y * 2 + core)

    def along_y(k):
        return (p, ((y + k) % SIDE) * 2 + r)

    def group(k):
        return pl.ds(((y + k) % SIDE) * 4, 4)

    sibling = (p, y * 2 + 1 - r)
    my_cols = pl.ds(pl.multiple_of(r * HALF, HALF), HALF)
    other_cols = pl.ds(pl.multiple_of((1 - r) * HALF, HALF), HALF)

    turns = (0, 1, 3, 2)

    def load(j):
        rows = pl.ds(pl.multiple_of(((y + turns[j]) % SIDE) * HALF, HALF), HALF)
        return pltpu.make_async_copy(proto.at[rows, my_cols], stage.at[j % 2], ld_sem.at[j])

    load(0).start()
    load(1).start()
    designs_in = [
        pltpu.make_async_copy(des.at[:, my_cols], des_m, des_sem.at[0]),
        pltpu.make_async_copy(des.at[:, other_cols], des_o, des_sem.at[1]),
    ]
    for c in designs_in:
        c.start()

    barrier = pltpu.get_barrier_semaphore()
    partners = [sibling]
    for k in (1, 2, 3):
        partners += [along_v(k, r), along_v(k, 1 - r), along_u(k, 1 - r), along_y(k)]
    partners += [along_u(1, r), along_u(3, r)]
    for q in partners:
        pl.semaphore_signal(barrier, inc=1, device_id=q, device_id_type=MESH)

    row = cand[...]
    col = to_column(row)
    same = (row >> 4) == (col >> 4)
    rank = jnp.sum(jnp.where(same & (iota((CANDS, CANDS), 1) < iota((CANDS, CANDS), 0)), 1, 0), axis=1, keepdims=True)
    slot = (col >> 4) * 2 + rank
    hit = slot == iota((CANDS, TILE), 1)
    wanted = jnp.sum(jnp.where(hit, (col & 15) + 1, 0), axis=0, keepdims=True) - 1
    req_v[...] = jnp.broadcast_to(wanted, (8, TILE))
    block = pos[...] >> 7
    spot = jnp.sum(jnp.where(col == block, slot, 0), axis=0, keepdims=True)
    prow[...] = spot * TILE + (pos[...] & 127)
    pltpu.make_async_copy(req_v, req_own, own_sem).start()

    pl.semaphore_wait(barrier, len(partners))

    req_in[0] = req_v[...]
    requests = [remote(req_v, req_in.at[1], rq_s.at[0], rq_r.at[1], sibling)]
    for k in (1, 2, 3):
        back = (SIDE - k) * 2
        requests.append(remote(req_v, req_in.at[back], rq_s.at[2 * k - 1], rq_r.at[back], along_v(k, r)))
        requests.append(remote(req_v, req_in.at[back + 1], rq_s.at[2 * k], rq_r.at[back + 1], along_u(k, 1 - r)))
    for c in requests:
        c.start()

    def own_chunk(k, way):
        low, count = ((0, 4), (2, 2), (0, 4), (0, 2))[k]
        part = pl.ds(((y + k) % SIDE) * 4 + low, count)
        dst = tab3 if way == 0 else tab1
        return remote(tab0.at[part], dst.at[part], ag_s.at[way, k], ag_r.at[way, k], along_u(1 if way == 0 else 3, r))

    for j in range(4):
        load(j).wait()
        for b in range(4):
            tab0[((y + turns[j]) % SIDE) * 4 + b] = stage[j % 2, TILE * b : TILE * (b + 1)].astype(BF16)
        if j < 2:
            own_chunk(turns[j], 0).start()
            own_chunk(turns[j], 1).start()
            load(j + 2).start()

    for c in designs_in:
        c.wait()

    @pl.loop(0, 4)
    def _(i):
        part = pl.ds(pl.multiple_of(i * COLS, COLS), COLS)
        dt_m[:, part] = des_m[part, :].T
        dt_o[:, part] = des_o[part, :].T

    for n in range(1, 8):
        remote(req_v, req_in.at[n], rq_s.at[0], rq_r.at[n], sibling).wait_recv()
    to_scalars = pltpu.make_async_copy(req_in, req_s, loc_sem.at[0])
    to_scalars.start()
    to_scalars.wait()

    def wanted_blocks(ku):
        first = owner(ku, 0) * 2
        for n in (0, 2, 3, 6, 7, 1, 4, 5):
            for i in range(2):
                val = tab[ku][jnp.maximum(req_s[n, 0, first + i], 0)]
                if n == 0:
                    arr_m[0, ku, i] = val
                else:
                    send[n, ku, i] = val
            if n:
                fetched(n, ku).start()

    def fetched(n, ku):
        k, so = n // 2, n % 2
        back = (SIDE - k) % SIDE
        if so == 0:
            return remote(send.at[n, ku], arr_m.at[back, ku], f_s.at[n, ku], fm_r.at[back, ku], along_v(k, r))
        return remote(send.at[n, ku], arr_o.at[back, ku], f_s.at[n, ku], fo_r.at[back, ku], along_v(k, 1 - r))

    def relay(way):
        part = pl.ds(4 * y + 2 * way, 2)
        src, to = (tab3, 1) if way == 0 else (tab1, 3)
        return remote(src.at[part], tab2.at[part], rl_s.at[way], rl_r.at[way], along_u(to, r))

    def share(k):
        return remote(tab2.at[group(0)], tab2.at[group(0)], gy_s.at[k], gy_r.at[SIDE - k], along_y(k))

    def hand(way, k):
        part = pl.ds(4 * y + (2 if k == 1 else 0), 2)
        src = tab3 if way == 0 else tab1
        return remote(src.at[part], src.at[part], ha_s.at[way, k // 2], ha_r.at[way, k // 2], along_y(k))

    for way in (0, 1):
        own_chunk(0, way).wait_recv()
        relay(way).start()
        hand(way, 1).start()
        hand(way, 3).start()
    for k in (3, 2):
        own_chunk(k, 0).start()
        own_chunk(k, 1).start()
    for way in (0, 1):
        relay(way).wait_recv()
    for k in (1, 3, 2):
        share(k).start()
    wanted_blocks(0)
    for way, ku in ((1, 1), (0, 3)):
        for k in (1, 2, 3):
            own_chunk(k, way).wait_recv()
        hand(way, 1).wait_recv()
        hand(way, 3).wait_recv()
        wanted_blocks(ku)
    for k in (1, 2, 3):
        remote(tab2.at[group(0)], tab2.at[group(0)], gy_s.at[k], gy_r.at[k], sibling).wait_recv()
    wanted_blocks(2)

    for ku in range(4):
        first = owner(ku, 0) * 2
        eye = iota((8, TILE), 1)
        reqs = req_in[:, 0, :]
        ids = [jnp.sum(jnp.where(eye == first + i, reqs, 0), axis=1, keepdims=True) for i in range(2)]
        ids = jnp.concatenate(ids, axis=0)
        place = iota((BLOCKS, 1), 0)
        entry = (place % 8) * 2 + place // 8
        key = ids * BLOCKS + entry
        rank = jnp.sum(jnp.where(to_row(key) < key, 1, 0), axis=1, keepdims=True)
        at = rank == iota((BLOCKS, TILE), 1)
        follows = jnp.sum(jnp.where((to_row(key) < key) & (to_row(ids) == ids), 1, 0), axis=1, keepdims=True)
        lane = iota((BLOCKS, TILE), 1)
        rows = [
            jnp.sum(jnp.where(at, entry, 0), axis=0, keepdims=True),
            jnp.sum(jnp.where(at & (follows == 0), 1, 0), axis=0, keepdims=True),
            jnp.maximum(jnp.sum(jnp.where(ids <= lane, 1, 0), axis=0, keepdims=True) - 1, 0),
            jnp.sum(jnp.where(ids == lane, 1, 0), axis=0, keepdims=True),
        ]
        for i in range(4):
            order_v[ku, i : i + 1, :] = rows[i]
    order_copy = pltpu.make_async_copy(order_v, order_s, loc_sem.at[1])
    order_copy.start()
    pltpu.make_async_copy(req_v, req_own, own_sem).wait()

    def logits_of(ku, kv, part):
        o = owner(ku, kv)
        left = jnp.dot(arr_m[kv, ku].reshape(PAIR, HALF), dt_m[:, part], preferred_element_type=F32)
        right = jnp.dot(arr_o[ku, kv].reshape(PAIR, HALF), dt_o[:, part], preferred_element_type=F32)
        rows = iota((PAIR, COLS), 0)
        held = jnp.where(rows < TILE, req_own[0, o * 2], req_own[0, o * 2 + 1]) >= 0
        target = rows + o * PAIR == prow[:, part]
        return jnp.where(held, (left + right) * D**-0.5, LOW), target

    m_run[...] = jnp.full((1, ROWS), LOW, F32)
    s_run[...] = jnp.zeros((1, ROWS), F32)
    pick[...] = jnp.zeros((1, ROWS), F32)

    @pl.loop(0, 16)
    def _(n):
        ku, kv = pair_of(n)

        @pl.when(kv != 0)
        def _():
            remote(send.at[1, 0], arr_m.at[kv, ku], f_s.at[1, 0], fm_r.at[kv, ku], sibling).wait_recv()

        remote(send.at[1, 0], arr_o.at[ku, kv], f_s.at[1, 0], fo_r.at[ku, kv], sibling).wait_recv()

        @pl.loop(0, ROWS // COLS)
        def _(i):
            part = pl.ds(pl.multiple_of(i * COLS, COLS), COLS)
            logits, target = logits_of(ku, kv, part)
            pick[:, part] += jnp.sum(jnp.where(target, logits, 0.0), axis=0, keepdims=True)
            before = m_run[:, part]
            now = jnp.maximum(before, jnp.max(logits, axis=0, keepdims=True))
            m_run[:, part] = now
            s_run[:, part] = s_run[:, part] * jnp.exp(before - now) + jnp.sum(jnp.exp(logits - now), axis=0, keepdims=True)

    total[...] = m_run[...] + jnp.log(s_run[...])
    loss_o[...] = total[...] - pick[...]

    for n in range(1, 8):
        for ku in range(4):
            fetched(n, ku).wait_send()
    for c in requests:
        c.wait_send()
    for k in range(4):
        own_chunk(k, 0).wait_send()
        own_chunk(k, 1).wait_send()
    for way in (0, 1):
        relay(way).wait_send()
        hand(way, 1).wait_send()
        hand(way, 3).wait_send()
    for k in (1, 2, 3):
        share(k).wait_send()

    def back_mine(ku, kv, k):
        back = (SIDE - kv) % SIDE
        return remote(send.at[kv * 2, ku], rr[k].at[pl.ds(back * 4, 2)], b_s.at[kv * 2, ku], b_r.at[k, back, 0], along_v(kv, r))

    def back_other(ku, kv, k):
        back = (SIDE - ku) % SIDE
        return remote(send.at[ku * 2 + 1, kv], rr[k].at[pl.ds(back * 4 + 2, 2)], b_s.at[ku * 2 + 1, kv], b_r.at[k, back, 1], along_u(ku, 1 - r))

    def second_pass(n):
        ku, kv = pair_of(15 - n)

        @pl.loop(0, ROWS // COLS)
        def _(i):
            part = pl.ds(pl.multiple_of(i * COLS, COLS), COLS)
            logits, target = logits_of(ku, kv, part)
            grads[kv, ku, :, part] = (jnp.exp(logits - total[:, part]) - jnp.where(target, 1.0, 0.0)).astype(BF16)

        mine = jnp.dot(grads[kv, ku], des_m[...], preferred_element_type=F32).astype(BF16).reshape(2, TILE, HALF)
        send[kv * 2, ku] = mine

        @pl.when((ku == 0) & (kv == 0))
        def _():
            rr[0][0:2] = send[0, 0]

        for k in (1, 2, 3):

            @pl.when((ku == k) & (kv == 0))
            def _():
                rr[k][0:2] = send[0, k]

            @pl.when((ku == k) & (kv != 0))
            def _():
                back_mine(ku, kv, k).start()

        other = jnp.dot(grads[kv, ku], des_o[...], preferred_element_type=F32).astype(BF16).reshape(2, TILE, HALF)
        send[ku * 2 + 1, kv] = other
        for k in (1, 2, 3):

            @pl.when(kv == k)
            def _():
                back_other(ku, kv, k).start()

    def sums(ku):
        for n in range(1, 8):
            k, so = n // 2, n % 2
            remote(send.at[1, 0], rr[ku].at[pl.ds(2 * n, 2)], b_s.at[1, 0], b_r.at[ku, k, so], sibling).wait_recv()

        @pl.loop(0, TILE // 16)
        def _(i):
            part = pl.ds(pl.multiple_of(i * 16, 16), 16)
            acc = jnp.zeros((16, HALF), F32)
            for t in range(BLOCKS):
                val = rr[ku][order_s[ku, 0, t], part, :].astype(F32)
                acc = jnp.where(order_s[ku, 1, t] == 1, val, acc + val)
                runs[t] = acc
            for j in range(BLOCKS):
                val = runs[order_s[ku, 2, j]]
                tab[ku][j, part, :] = jnp.where(order_s[ku, 3, j] > 0, val, 0.0).astype(BF16)

    def design_grad(q, h):
        part = pl.ds(q * COLS, COLS)
        acc = stage.at[0, pl.ds(0, COLS)]
        acc[...] = jnp.zeros((COLS, HALF), F32)

        @pl.loop(0, 4)
        def _(k):
            lhs = grads[k, :, :, part] if h == 0 else grads[:, k, :, part]
            rhs = arr_m[k] if h == 0 else arr_o[k]
            acc[...] += lax.dot_general(
                lhs.reshape(ROWS, COLS), rhs.reshape(ROWS, HALF), (((0,), (0,)), ((), ())), preferred_element_type=F32
            )

        dg_s[q, h] = acc[...].astype(BF16)
        dg_out(q, h).start()

    def dg_out(q, h):
        cols = my_cols if h == 0 else other_cols
        return pltpu.make_async_copy(dg_s.at[q, h], dg_o.at[pl.ds(q * COLS, COLS), cols], out_sem.at[q, h])

    def far_along_y(k):
        return remote(tab2.at[group(k)], far_y.at[SIDE - k], fy_s.at[k], fy_r.at[SIDE - k], along_y(k))

    def far(way):
        part = pl.ds(4 * y + 2 * way, 2)
        return remote(tab2.at[part], merge.at[way], mg_s.at[way], mg_r.at[way], along_u(1 if way == 0 else 3, r))

    def given(way):
        return from_y.at[0] if way == 0 else far_y.at[0]

    def give(way, k):
        low = 0 if k == 1 else 2
        part = pl.ds(((y + k) % SIDE) * 4 + low, 2)
        src = tab1 if way == 0 else tab3
        return remote(src.at[part], given(way).at[pl.ds(low, 2)], gv_s.at[way, k // 2], gv_r.at[way, k // 2], along_y(k))

    kept = ((0, 4), (2, 2), (0, 4), (0, 2))

    def near(k, way):
        low, count = kept[k]
        part, here = pl.ds(((y + k) % SIDE) * 4 + low, count), pl.ds(low, count)
        if way == 0:
            return remote(tab1.at[part], from_down.at[k, here], rs_s.at[0, k], rs_r.at[0, k], along_u(1, r))
        return remote(tab3.at[part], from_up.at[k, here], rs_s.at[1, k], rs_r.at[1, k], along_u(3, r))

    def to_y(k):
        return remote(tab0.at[group(k)], from_y.at[SIDE - k], y_s.at[k], y_r.at[SIDE - k], along_y(k))

    pl.loop(0, 12)(second_pass)
    order_copy.wait()
    sums(2)
    for k in (1, 3, 2):
        far_along_y(k).start()
    pl.loop(12, 16)(second_pass)
    for kv in (1, 3, 2):
        back_mine(0, kv, 0).start()
    design_grad(0, 0)
    for way, ku in ((1, 3), (0, 1)):
        sums(ku)
        give(way, 1).start()
        give(way, 3).start()
        near(2, way).start()
    for ku in (0, 1, 3, 2):
        back_other(ku, 0, 0).start()
    for k in (1, 3):
        near(k, 1).start()
        near(k, 0).start()
    design_grad(0, 1)
    design_grad(1, 0)
    for k in (1, 3, 2):
        remote(tab2.at[group(0)], far_y.at[k], fy_s.at[k], fy_r.at[k], sibling).wait_recv()
    for b in range(4):
        val = tab2[4 * y + b].astype(F32)
        for k in (1, 2, 3):
            val += far_y[k, b].astype(F32)
        tab2[4 * y + b] = val.astype(BF16)
    far(0).start()
    far(1).start()
    design_grad(1, 1)
    sums(0)

    def add_near(k):
        near(k, 0).wait_recv()
        near(k, 1).wait_recv()
        low, count = kept[k]
        for b in range(low, low + count):
            at = ((y + k) % SIDE) * 4 + b
            val = tab0[at].astype(F32) + from_up[k, b].astype(F32) + from_down[k, b].astype(F32)
            tab0[at] = val.astype(BF16)

    add_near(2)
    to_y(2).start()
    design_grad(2, 0)
    add_near(1)
    to_y(1).start()
    design_grad(2, 1)
    add_near(3)
    to_y(3).start()
    for way in (0, 1):
        src = tab1 if way == 0 else tab3
        give(way, 1).wait_recv()
        give(way, 3).wait_recv()
        far(way).wait_recv()
        for b in range(4):
            val = src[4 * y + b].astype(F32) + given(way)[b].astype(F32)
            if b // 2 == way:
                val += merge[way, b % 2].astype(F32)
            src[4 * y + b] = val.astype(BF16)
        near(0, way).start()
    design_grad(3, 0)
    design_grad(3, 1)
    add_near(0)
    for k in (1, 3, 2):
        remote(tab0.at[pl.ds(0, 4)], from_y.at[k], y_s.at[0], y_r.at[k], sibling).wait_recv()

    def reduced(b):
        val = tab0[4 * y + b].astype(F32)
        for k in (1, 2, 3):
            val += from_y[k, b].astype(F32)
        return val

    for i in range(2):
        stage[1, pl.ds(PAIR + i * TILE, TILE)] = reduced(2 * (1 - r) + i)
    cross = remote(stage.at[1, pl.ds(PAIR, PAIR)], core_in, c_s, c_r, sibling)
    cross.start()
    for i in range(2):
        stage[1, pl.ds(i * TILE, TILE)] = reduced(2 * r + i)
    outs = [pltpu.make_async_copy(stage.at[1, pl.ds(0, PAIR)], pg_o.at[:, my_cols], loc_sem.at[2])]
    outs[0].start()
    cross.wait_recv()
    outs.append(pltpu.make_async_copy(core_in, pg_o.at[:, other_cols], loc_sem.at[3]))
    outs[1].start()

    for kv in range(4):
        for ku in range(4):
            if kv:
                back_mine(ku, kv, ku).wait_send()
            back_other(ku, kv, kv).wait_send()
    for k in range(4):
        near(k, 0).wait_send()
        near(k, 1).wait_send()
        if k:
            far_along_y(k).wait_send()
            to_y(k).wait_send()
        for h in range(2):
            dg_out(k, h).wait()
    for way in (0, 1):
        far(way).wait_send()
        give(way, 1).wait_send()
        give(way, 3).wait_send()
    cross.wait_send()
    for c in outs:
        c.wait()


def settle(losses, design_grad, proto_grad, losses_o, design_grad_o, proto_grad_o, one, many, few, sems):
    moves = [(losses, one, losses_o)]
    for i in range(4):
        part = pl.ds(i * COLS, COLS)
        moves.append((design_grad.at[part], many.at[part], design_grad_o.at[part]))
    for i in range(2):
        part = pl.ds(i * TILE, TILE)
        moves.append((proto_grad.at[part], few.at[part], proto_grad_o.at[part]))
    reads = [pltpu.make_async_copy(a, b, sems.at[0, n]) for n, (a, b, c) in enumerate(moves)]
    writes = [pltpu.make_async_copy(b, c, sems.at[1, n]) for n, (a, b, c) in enumerate(moves)]
    for c in reads:
        c.start()
    for a, b in zip(reads, writes):
        a.wait()
        b.start()
    for c in writes:
        c.wait()


def body(designs, prototypes, candidates, positives):
    vmem = lambda shape, dtype: pltpu.VMEM(shape, dtype)
    dma = lambda *shape: pltpu.SemaphoreType.DMA(shape)
    blocks = (BLOCKS, TILE, HALF)
    pairs = (SIDE, SIDE, 2, TILE, HALF)
    losses, design_grad, proto_grad = pl.pallas_call(
        kernel,
        out_shape=(
            jax.ShapeDtypeStruct((1, ROWS), F32),
            jax.ShapeDtypeStruct((ROWS, D), BF16),
            jax.ShapeDtypeStruct((PAIR, D), F32),
        ),
        in_specs=[
            pl.BlockSpec(memory_space=pl.ANY),
            pl.BlockSpec(memory_space=pl.ANY),
            pl.BlockSpec(memory_space=pltpu.VMEM),
            pl.BlockSpec(memory_space=pltpu.VMEM),
        ],
        out_specs=(
            pl.BlockSpec(memory_space=pltpu.VMEM),
            pl.BlockSpec(memory_space=pl.ANY),
            pl.BlockSpec(memory_space=pl.ANY),
        ),
        scratch_shapes=[
            *[vmem(blocks, BF16) for _ in range(8)],
            vmem((8, SIDE, 2, TILE, HALF), BF16),
            vmem(pairs, BF16),
            vmem(pairs, BF16),
            vmem((ROWS, HALF), BF16),
            vmem((ROWS, HALF), BF16),
            vmem((HALF, ROWS), BF16),
            vmem((HALF, ROWS), BF16),
            vmem((SIDE, SIDE, PAIR, ROWS), BF16),
            vmem((2, HALF, HALF), F32),
            vmem((2, 2, TILE, HALF), BF16),
            vmem((4, 4, TILE, HALF), BF16),
            vmem((4, 4, TILE, HALF), BF16),
            vmem((4, 4, TILE, HALF), BF16),
            vmem((4, 4, TILE, HALF), BF16),
            vmem((BLOCKS, 16, HALF), F32),
            vmem((PAIR, HALF), F32),
            vmem((4, 2, COLS, HALF), BF16),
            vmem((1, ROWS), I32),
            *[vmem((1, ROWS), F32) for _ in range(4)],
            vmem((8, TILE), I32),
            vmem((8, 8, TILE), I32),
            vmem((4, 8, TILE), I32),
            pltpu.SMEM((8, TILE), I32),
            pltpu.SMEM((8, 8, TILE), I32),
            pltpu.SMEM((4, 8, TILE), I32),
            dma(4),
            dma(2),
            dma(4, 2),
            dma(4),
            pltpu.SemaphoreType.DMA,
            dma(8),
            dma(8),
            dma(2, 4),
            dma(2, 4),
            dma(2),
            dma(2),
            dma(4),
            dma(4),
            dma(2, 2),
            dma(2, 2),
            dma(8, 4),
            dma(4, 4),
            dma(4, 4),
            dma(8, 4),
            dma(4, 4, 2),
            dma(4),
            dma(4),
            dma(2, 2),
            dma(2, 2),
            dma(2),
            dma(2),
            dma(2, 4),
            dma(2, 4),
            dma(4),
            dma(4),
            pltpu.SemaphoreType.DMA,
            pltpu.SemaphoreType.DMA,
        ],
        compiler_params=pltpu.CompilerParams(
            collective_id=0, has_side_effects=True, vmem_limit_bytes=62 * 2**20
        ),
    )(designs, prototypes, candidates, positives.reshape(1, ROWS))
    losses, design_grad, proto_grad = pl.pallas_call(
        settle,
        out_shape=(
            jax.ShapeDtypeStruct((1, ROWS), F32),
            jax.ShapeDtypeStruct((ROWS, D), BF16),
            jax.ShapeDtypeStruct((PAIR, D), F32),
        ),
        in_specs=[pl.BlockSpec(memory_space=pl.ANY)] * 3,
        out_specs=(pl.BlockSpec(memory_space=pl.ANY),) * 3,
        scratch_shapes=[vmem((1, ROWS), F32), vmem((ROWS, D), BF16), vmem((PAIR, D), F32), dma(2, 7)],
    )(losses, design_grad, proto_grad)
    return losses.reshape(ROWS), design_grad, proto_grad


def solution(mesh):
    return jax.shard_map(
        body,
        mesh=mesh,
        in_specs=(
            P(("proto", "design"), None),
            P("proto", None),
            P(("proto", "design"), None),
            P(("proto", "design")),
        ),
        out_specs=(
            P(("proto", "design")),
            P(("proto", "design"), None),
            P(("proto", "design"), None),
        ),
        check_vma=False,
    )
```

```python
import jax
import jax.numpy as jnp
from jax import lax
from jax.experimental import pallas as pl
from jax.experimental.pallas import tpu as pltpu
from jax.sharding import PartitionSpec as P

D = 1024
HALF = 512
TILE = 128
ROWS = 1024
SIDE = 4
BLOCKS = 16
CANDS = 24
PAIR = 2 * TILE
COLS = 256
LOW = -3.0e38
MESH = pl.DeviceIdType.MESH
BF16 = jnp.bfloat16
F32 = jnp.float32
I32 = jnp.int32


def remote(src, dst, send_sem, recv_sem, device):
    return pltpu.make_async_remote_copy(
        src_ref=src, dst_ref=dst, send_sem=send_sem, recv_sem=recv_sem, device_id=device, device_id_type=MESH
    )


def iota(shape, dim):
    return lax.broadcasted_iota(I32, shape, dim)


def to_column(row):
    n = row.shape[1]
    return jnp.sum(jnp.where(iota((n, n), 0) == iota((n, n), 1), jnp.broadcast_to(row, (n, n)), 0), axis=1, keepdims=True)


def to_row(col):
    n = col.shape[0]
    return jnp.sum(jnp.where(iota((n, n), 0) == iota((n, n), 1), jnp.broadcast_to(col, (n, n)), 0), axis=0, keepdims=True)


def gray(k):
    return k + (k // 2) * (1 - 2 * (k % 2))


def pair_of(n):
    s = jnp.where(n >= 1, 1, 0) + jnp.where(n >= 4, 1, 0) + jnp.where(n >= 9, 1, 0)
    m = n - s * s
    odd = m % 2
    return gray(s + odd * (m // 2 - s)), gray(m // 2 + odd * (s - m // 2))


def kernel(
    des, proto, cand, pos, loss_o, dg_o, pg_o,
    tab0, tab1, tab2, tab3, rr0, rr1, rr2, rr3,
    send, arr_m, arr_o, des_m, des_o, dt_m, dt_o, grads, stage, merge, from_up, from_down, from_y, far_y, runs, core_in, dg_s,
    prow, m_run, s_run, pick, total, req_v, req_in, order_v, req_own, req_s, order_s,
    ld_sem, des_sem, out_sem, loc_sem, own_sem, rq_s, rq_r, ag_s, ag_r, rl_s, rl_r, gy_s, gy_r, ha_s, ha_r, f_s, fm_r, fo_r, b_s, b_r,
    fy_s, fy_r, mg_s, mg_r, rs_s, rs_r, y_s, y_r, c_s, c_r,
):
    p, d = lax.axis_index("proto"), lax.axis_index("design")
    x, z, y, r = p // SIDE, p % SIDE, d // 2, d % 2
    tab, rr = (tab0, tab1, tab2, tab3), (rr0, rr1, rr2, rr3)

    def owner(ku, kv):
        return ((x + ku * (1 - r) + kv * r) % SIDE) * SIDE + (z + ku * r + kv * (1 - r)) % SIDE

    def along_u(k, core):
        return (owner(k, 0), y * 2 + core)

    def along_v(k, core):
        return (owner(0, k), y * 2 + core)

    def along_y(k):
        return (p, ((y + k) % SIDE) * 2 + r)

    def group(k):
        return pl.ds(((y + k) % SIDE) * 4, 4)

    sibling = (p, y * 2 + 1 - r)
    my_cols = pl.ds(pl.multiple_of(r * HALF, HALF), HALF)
    other_cols = pl.ds(pl.multiple_of((1 - r) * HALF, HALF), HALF)

    turns = (0, 1, 3, 2)

    def load(j):
        rows = pl.ds(pl.multiple_of(((y + turns[j]) % SIDE) * HALF, HALF), HALF)
        return pltpu.make_async_copy(proto.at[rows, my_cols], stage.at[j % 2], ld_sem.at[j])

    load(0).start()
    load(1).start()
    designs_in = [
        pltpu.make_async_copy(des.at[:, my_cols], des_m, des_sem.at[0]),
        pltpu.make_async_copy(des.at[:, other_cols], des_o, des_sem.at[1]),
    ]
    for c in designs_in:
        c.start()

    barrier = pltpu.get_barrier_semaphore()
    partners = [sibling]
    for k in (1, 2, 3):
        partners += [along_v(k, r), along_v(k, 1 - r), along_u(k, 1 - r), along_y(k)]
    partners += [along_u(1, r), along_u(3, r)]
    for q in partners:
        pl.semaphore_signal(barrier, inc=1, device_id=q, device_id_type=MESH)

    row = cand[...]
    col = to_column(row)
    same = (row >> 4) == (col >> 4)
    rank = jnp.sum(jnp.where(same & (iota((CANDS, CANDS), 1) < iota((CANDS, CANDS), 0)), 1, 0), axis=1, keepdims=True)
    slot = (col >> 4) * 2 + rank
    hit = slot == iota((CANDS, TILE), 1)
    wanted = jnp.sum(jnp.where(hit, (col & 15) + 1, 0), axis=0, keepdims=True) - 1
    req_v[...] = jnp.broadcast_to(wanted, (8, TILE))
    block = pos[...] >> 7
    spot = jnp.sum(jnp.where(col == block, slot, 0), axis=0, keepdims=True)
    prow[...] = spot * TILE + (pos[...] & 127)
    pltpu.make_async_copy(req_v, req_own, own_sem).start()

    pl.semaphore_wait(barrier, len(partners))

    req_in[0] = req_v[...]
    requests = [remote(req_v, req_in.at[1], rq_s.at[0], rq_r.at[1], sibling)]
    for k in (1, 2, 3):
        back = (SIDE - k) * 2
        requests.append(remote(req_v, req_in.at[back], rq_s.at[2 * k - 1], rq_r.at[back], along_v(k, r)))
        requests.append(remote(req_v, req_in.at[back + 1], rq_s.at[2 * k], rq_r.at[back + 1], along_u(k, 1 - r)))
    for c in requests:
        c.start()

    def own_chunk(k, way):
        low, count = ((0, 4), (2, 2), (0, 4), (0, 2))[k]
        part = pl.ds(((y + k) % SIDE) * 4 + low, count)
        dst = tab3 if way == 0 else tab1
        return remote(tab0.at[part], dst.at[part], ag_s.at[way, k], ag_r.at[way, k], along_u(1 if way == 0 else 3, r))

    for j in range(4):
        load(j).wait()
        for b in range(4):
            tab0[((y + turns[j]) % SIDE) * 4 + b] = stage[j % 2, TILE * b : TILE * (b + 1)].astype(BF16)
        if j < 2:
            own_chunk(turns[j], 0).start()
            own_chunk(turns[j], 1).start()
            load(j + 2).start()

    for c in designs_in:
        c.wait()

    @pl.loop(0, 4)
    def _(i):
        part = pl.ds(pl.multiple_of(i * COLS, COLS), COLS)
        dt_m[:, part] = des_m[part, :].T
        dt_o[:, part] = des_o[part, :].T

    for n in range(1, 8):
        remote(req_v, req_in.at[n], rq_s.at[0], rq_r.at[n], sibling).wait_recv()
    to_scalars = pltpu.make_async_copy(req_in, req_s, loc_sem.at[0])
    to_scalars.start()
    to_scalars.wait()

    def wanted_blocks(ku):
        first = owner(ku, 0) * 2
        for n in (0, 2, 3, 6, 7, 1, 4, 5):
            for i in range(2):
                val = tab[ku][jnp.maximum(req_s[n, 0, first + i], 0)]
                if n == 0:
                    arr_m[0, ku, i] = val
                else:
                    send[n, ku, i] = val
            if n:
                fetched(n, ku).start()

    def fetched(n, ku):
        k, so = n // 2, n % 2
        back = (SIDE - k) % SIDE
        if so == 0:
            return remote(send.at[n, ku], arr_m.at[back, ku], f_s.at[n, ku], fm_r.at[back, ku], along_v(k, r))
        return remote(send.at[n, ku], arr_o.at[back, ku], f_s.at[n, ku], fo_r.at[back, ku], along_v(k, 1 - r))

    def relay(way):
        part = pl.ds(4 * y + 2 * way, 2)
        src, to = (tab3, 1) if way == 0 else (tab1, 3)
        return remote(src.at[part], tab2.at[part], rl_s.at[way], rl_r.at[way], along_u(to, r))

    def share(k):
        return remote(tab2.at[group(0)], tab2.at[group(0)], gy_s.at[k], gy_r.at[SIDE - k], along_y(k))

    def hand(way, k):
        part = pl.ds(4 * y + (2 if k == 1 else 0), 2)
        src = tab3 if way == 0 else tab1
        return remote(src.at[part], src.at[part], ha_s.at[way, k // 2], ha_r.at[way, k // 2], along_y(k))

    for way in (0, 1):
        own_chunk(0, way).wait_recv()
        relay(way).start()
        hand(way, 1).start()
        hand(way, 3).start()
    for k in (3, 2):
        own_chunk(k, 0).start()
        own_chunk(k, 1).start()
    wanted_blocks(0)
    for way in (0, 1):
        relay(way).wait_recv()
    for k in (1, 3, 2):
        share(k).start()
    for way, ku in ((1, 1), (0, 3)):
        for k in (1, 2, 3):
            own_chunk(k, way).wait_recv()
        hand(way, 1).wait_recv()
        hand(way, 3).wait_recv()
        wanted_blocks(ku)
    for k in (1, 2, 3):
        remote(tab2.at[group(0)], tab2.at[group(0)], gy_s.at[k], gy_r.at[k], sibling).wait_recv()
    wanted_blocks(2)

    for ku in range(4):
        first = owner(ku, 0) * 2
        eye = iota((8, TILE), 1)
        reqs = req_in[:, 0, :]
        ids = [jnp.sum(jnp.where(eye == first + i, reqs, 0), axis=1, keepdims=True) for i in range(2)]
        ids = jnp.concatenate(ids, axis=0)
        place = iota((BLOCKS, 1), 0)
        entry = (place % 8) * 2 + place // 8
        key = ids * BLOCKS + entry
        rank = jnp.sum(jnp.where(to_row(key) < key, 1, 0), axis=1, keepdims=True)
        at = rank == iota((BLOCKS, TILE), 1)
        follows = jnp.sum(jnp.where((to_row(key) < key) & (to_row(ids) == ids), 1, 0), axis=1, keepdims=True)
        lane = iota((BLOCKS, TILE), 1)
        rows = [
            jnp.sum(jnp.where(at, entry, 0), axis=0, keepdims=True),
            jnp.sum(jnp.where(at & (follows == 0), 1, 0), axis=0, keepdims=True),
            jnp.maximum(jnp.sum(jnp.where(ids <= lane, 1, 0), axis=0, keepdims=True) - 1, 0),
            jnp.sum(jnp.where(ids == lane, 1, 0), axis=0, keepdims=True),
        ]
        for i in range(4):
            order_v[ku, i : i + 1, :] = rows[i]
    order_copy = pltpu.make_async_copy(order_v, order_s, loc_sem.at[1])
    order_copy.start()
    pltpu.make_async_copy(req_v, req_own, own_sem).wait()

    def logits_of(ku, kv, part):
        o = owner(ku, kv)
        left = jnp.dot(arr_m[kv, ku].reshape(PAIR, HALF), dt_m[:, part], preferred_element_type=F32)
        right = jnp.dot(arr_o[ku, kv].reshape(PAIR, HALF), dt_o[:, part], preferred_element_type=F32)
        rows = iota((PAIR, COLS), 0)
        held = jnp.where(rows < TILE, req_own[0, o * 2], req_own[0, o * 2 + 1]) >= 0
        target = rows + o * PAIR == prow[:, part]
        return jnp.where(held, (left + right) * D**-0.5, LOW), target

    m_run[...] = jnp.full((1, ROWS), LOW, F32)
    s_run[...] = jnp.zeros((1, ROWS), F32)
    pick[...] = jnp.zeros((1, ROWS), F32)

    @pl.loop(0, 16)
    def _(n):
        ku, kv = pair_of(n)

        @pl.when(kv != 0)
        def _():
            remote(send.at[1, 0], arr_m.at[kv, ku], f_s.at[1, 0], fm_r.at[kv, ku], sibling).wait_recv()

        remote(send.at[1, 0], arr_o.at[ku, kv], f_s.at[1, 0], fo_r.at[ku, kv], sibling).wait_recv()

        @pl.loop(0, ROWS // COLS)
        def _(i):
            part = pl.ds(pl.multiple_of(i * COLS, COLS), COLS)
            logits, target = logits_of(ku, kv, part)
            pick[:, part] += jnp.sum(jnp.where(target, logits, 0.0), axis=0, keepdims=True)
            before = m_run[:, part]
            now = jnp.maximum(before, jnp.max(logits, axis=0, keepdims=True))
            m_run[:, part] = now
            s_run[:, part] = s_run[:, part] * jnp.exp(before - now) + jnp.sum(jnp.exp(logits - now), axis=0, keepdims=True)

    total[...] = m_run[...] + jnp.log(s_run[...])
    loss_o[...] = total[...] - pick[...]

    for n in range(1, 8):
        for ku in range(4):
            fetched(n, ku).wait_send()
    for c in requests:
        c.wait_send()
    for k in range(4):
        own_chunk(k, 0).wait_send()
        own_chunk(k, 1).wait_send()
    for way in (0, 1):
        relay(way).wait_send()
        hand(way, 1).wait_send()
        hand(way, 3).wait_send()
    for k in (1, 2, 3):
        share(k).wait_send()

    def back_mine(ku, kv, k):
        back = (SIDE - kv) % SIDE
        return remote(send.at[kv * 2, ku], rr[k].at[pl.ds(back * 4, 2)], b_s.at[kv * 2, ku], b_r.at[k, back, 0], along_v(kv, r))

    def back_other(ku, kv, k):
        back = (SIDE - ku) % SIDE
        return remote(send.at[ku * 2 + 1, kv], rr[k].at[pl.ds(back * 4 + 2, 2)], b_s.at[ku * 2 + 1, kv], b_r.at[k, back, 1], along_u(ku, 1 - r))

    def second_pass(n):
        ku, kv = pair_of(15 - n)

        @pl.loop(0, ROWS // COLS)
        def _(i):
            part = pl.ds(pl.multiple_of(i * COLS, COLS), COLS)
            logits, target = logits_of(ku, kv, part)
            grads[kv, ku, :, part] = (jnp.exp(logits - total[:, part]) - jnp.where(target, 1.0, 0.0)).astype(BF16)

        mine = jnp.dot(grads[kv, ku], des_m[...], preferred_element_type=F32).astype(BF16).reshape(2, TILE, HALF)
        send[kv * 2, ku] = mine
        other = jnp.dot(grads[kv, ku], des_o[...], preferred_element_type=F32).astype(BF16).reshape(2, TILE, HALF)
        send[ku * 2 + 1, kv] = other

        @pl.when((ku == 0) & (kv == 0))
        def _():
            rr[0][0:2] = send[0, 0]

        for k in (1, 2, 3):

            @pl.when((ku == k) & (kv == 0))
            def _():
                rr[k][0:2] = send[0, k]

            @pl.when((ku == k) & (kv != 0))
            def _():
                back_mine(ku, kv, k).start()

            @pl.when(kv == k)
            def _():
                back_other(ku, kv, k).start()

    def sums(ku):
        for n in range(1, 8):
            k, so = n // 2, n % 2
            remote(send.at[1, 0], rr[ku].at[pl.ds(2 * n, 2)], b_s.at[1, 0], b_r.at[ku, k, so], sibling).wait_recv()

        @pl.loop(0, TILE // 16)
        def _(i):
            part = pl.ds(pl.multiple_of(i * 16, 16), 16)
            acc = jnp.zeros((16, HALF), F32)
            for t in range(BLOCKS):
                val = rr[ku][order_s[ku, 0, t], part, :].astype(F32)
                acc = jnp.where(order_s[ku, 1, t] == 1, val, acc + val)
                runs[t] = acc
            for j in range(BLOCKS):
                val = runs[order_s[ku, 2, j]]
                tab[ku][j, part, :] = jnp.where(order_s[ku, 3, j] > 0, val, 0.0).astype(BF16)

    def design_grad(q, h):
        part = pl.ds(q * COLS, COLS)
        acc = stage.at[0, pl.ds(0, COLS)]
        acc[...] = jnp.zeros((COLS, HALF), F32)

        @pl.loop(0, 4)
        def _(k):
            lhs = grads[k, :, :, part] if h == 0 else grads[:, k, :, part]
            rhs = arr_m[k] if h == 0 else arr_o[k]
            acc[...] += lax.dot_general(
                lhs.reshape(ROWS, COLS), rhs.reshape(ROWS, HALF), (((0,), (0,)), ((), ())), preferred_element_type=F32
            )

        dg_s[q, h] = acc[...].astype(BF16)
        dg_out(q, h).start()

    def dg_out(q, h):
        cols = my_cols if h == 0 else other_cols
        return pltpu.make_async_copy(dg_s.at[q, h], dg_o.at[pl.ds(q * COLS, COLS), cols], out_sem.at[q, h])

    def far_along_y(k):
        return remote(tab2.at[group(k)], far_y.at[SIDE - k], fy_s.at[k], fy_r.at[SIDE - k], along_y(k))

    def far(way):
        part = pl.ds(4 * y + 2 * way, 2)
        return remote(tab2.at[part], merge.at[way], mg_s.at[way], mg_r.at[way], along_u(1 if way == 0 else 3, r))

    def near(k, way):
        if way == 0:
            return remote(tab1.at[group(k)], from_down.at[k], rs_s.at[0, k], rs_r.at[0, k], along_u(1, r))
        return remote(tab3.at[group(k)], from_up.at[k], rs_s.at[1, k], rs_r.at[1, k], along_u(3, r))

    def to_y(k):
        return remote(tab0.at[group(k)], from_y.at[SIDE - k], y_s.at[k], y_r.at[SIDE - k], along_y(k))

    pl.loop(0, 12)(second_pass)
    order_copy.wait()
    sums(2)
    for k in (1, 3, 2):
        far_along_y(k).start()
    pl.loop(12, 16)(second_pass)
    for kv in (1, 3, 2):
        back_mine(0, kv, 0).start()
    for ku in (0, 1, 3, 2):
        back_other(ku, 0, 0).start()
    design_grad(0, 0)
    sums(3)
    near(2, 1).start()
    sums(1)
    near(2, 0).start()
    for k in (1, 3):
        near(k, 1).start()
        near(k, 0).start()
    design_grad(0, 1)
    design_grad(1, 0)
    for k in (1, 3, 2):
        remote(tab2.at[group(0)], far_y.at[k], fy_s.at[k], fy_r.at[k], sibling).wait_recv()
    for b in range(4):
        val = tab2[4 * y + b].astype(F32)
        for k in (1, 2, 3):
            val += far_y[k, b].astype(F32)
        tab2[4 * y + b] = val.astype(BF16)
    far(0).start()
    far(1).start()
    design_grad(1, 1)
    sums(0)

    def add_near(k):
        near(k, 0).wait_recv()
        near(k, 1).wait_recv()
        for b in range(4):
            at = ((y + k) % SIDE) * 4 + b
            val = tab0[at].astype(F32) + from_up[k, b].astype(F32) + from_down[k, b].astype(F32)
            tab0[at] = val.astype(BF16)

    add_near(2)
    to_y(2).start()
    design_grad(2, 0)
    add_near(1)
    to_y(1).start()
    design_grad(2, 1)
    add_near(3)
    to_y(3).start()
    for way in (0, 1):
        src = tab1 if way == 0 else tab3
        far(way).wait_recv()
        for b in range(2):
            at = 4 * y + 2 * way + b
            src[at] = (src[at].astype(F32) + merge[way, b].astype(F32)).astype(BF16)
        near(0, way).start()
    design_grad(3, 0)
    design_grad(3, 1)
    add_near(0)
    for k in (1, 3, 2):
        remote(tab0.at[pl.ds(0, 4)], from_y.at[k], y_s.at[0], y_r.at[k], sibling).wait_recv()

    def reduced(b):
        val = tab0[4 * y + b].astype(F32)
        for k in (1, 2, 3):
            val += from_y[k, b].astype(F32)
        return val

    for i in range(2):
        stage[1, pl.ds(PAIR + i * TILE, TILE)] = reduced(2 * (1 - r) + i)
    cross = remote(stage.at[1, pl.ds(PAIR, PAIR)], core_in, c_s, c_r, sibling)
    cross.start()
    for i in range(2):
        stage[1, pl.ds(i * TILE, TILE)] = reduced(2 * r + i)
    outs = [pltpu.make_async_copy(stage.at[1, pl.ds(0, PAIR)], pg_o.at[:, my_cols], loc_sem.at[2])]
    outs[0].start()
    cross.wait_recv()
    outs.append(pltpu.make_async_copy(core_in, pg_o.at[:, other_cols], loc_sem.at[3]))
    outs[1].start()

    for kv in range(4):
        for ku in range(4):
            if kv:
                back_mine(ku, kv, ku).wait_send()
            back_other(ku, kv, kv).wait_send()
    for k in range(4):
        near(k, 0).wait_send()
        near(k, 1).wait_send()
        if k:
            far_along_y(k).wait_send()
            to_y(k).wait_send()
        for h in range(2):
            dg_out(k, h).wait()
    far(0).wait_send()
    far(1).wait_send()
    cross.wait_send()
    for c in outs:
        c.wait()


def settle(losses, design_grad, proto_grad, losses_o, design_grad_o, proto_grad_o, one, many, few, sems):
    moves = [(losses, one, losses_o)]
    for i in range(4):
        part = pl.ds(i * COLS, COLS)
        moves.append((design_grad.at[part], many.at[part], design_grad_o.at[part]))
    for i in range(2):
        part = pl.ds(i * TILE, TILE)
        moves.append((proto_grad.at[part], few.at[part], proto_grad_o.at[part]))
    reads = [pltpu.make_async_copy(a, b, sems.at[0, n]) for n, (a, b, c) in enumerate(moves)]
    writes = [pltpu.make_async_copy(b, c, sems.at[1, n]) for n, (a, b, c) in enumerate(moves)]
    for c in reads:
        c.start()
    for a, b in zip(reads, writes):
        a.wait()
        b.start()
    for c in writes:
        c.wait()


def body(designs, prototypes, candidates, positives):
    vmem = lambda shape, dtype: pltpu.VMEM(shape, dtype)
    dma = lambda *shape: pltpu.SemaphoreType.DMA(shape)
    blocks = (BLOCKS, TILE, HALF)
    pairs = (SIDE, SIDE, 2, TILE, HALF)
    losses, design_grad, proto_grad = pl.pallas_call(
        kernel,
        out_shape=(
            jax.ShapeDtypeStruct((1, ROWS), F32),
            jax.ShapeDtypeStruct((ROWS, D), BF16),
            jax.ShapeDtypeStruct((PAIR, D), F32),
        ),
        in_specs=[
            pl.BlockSpec(memory_space=pl.ANY),
            pl.BlockSpec(memory_space=pl.ANY),
            pl.BlockSpec(memory_space=pltpu.VMEM),
            pl.BlockSpec(memory_space=pltpu.VMEM),
        ],
        out_specs=(
            pl.BlockSpec(memory_space=pltpu.VMEM),
            pl.BlockSpec(memory_space=pl.ANY),
            pl.BlockSpec(memory_space=pl.ANY),
        ),
        scratch_shapes=[
            *[vmem(blocks, BF16) for _ in range(8)],
            vmem((8, SIDE, 2, TILE, HALF), BF16),
            vmem(pairs, BF16),
            vmem(pairs, BF16),
            vmem((ROWS, HALF), BF16),
            vmem((ROWS, HALF), BF16),
            vmem((HALF, ROWS), BF16),
            vmem((HALF, ROWS), BF16),
            vmem((SIDE, SIDE, PAIR, ROWS), BF16),
            vmem((2, HALF, HALF), F32),
            vmem((2, 2, TILE, HALF), BF16),
            vmem((4, 4, TILE, HALF), BF16),
            vmem((4, 4, TILE, HALF), BF16),
            vmem((4, 4, TILE, HALF), BF16),
            vmem((4, 4, TILE, HALF), BF16),
            vmem((BLOCKS, 16, HALF), F32),
            vmem((PAIR, HALF), F32),
            vmem((4, 2, COLS, HALF), BF16),
            vmem((1, ROWS), I32),
            *[vmem((1, ROWS), F32) for _ in range(4)],
            vmem((8, TILE), I32),
            vmem((8, 8, TILE), I32),
            vmem((4, 8, TILE), I32),
            pltpu.SMEM((8, TILE), I32),
            pltpu.SMEM((8, 8, TILE), I32),
            pltpu.SMEM((4, 8, TILE), I32),
            dma(4),
            dma(2),
            dma(4, 2),
            dma(4),
            pltpu.SemaphoreType.DMA,
            dma(8),
            dma(8),
            dma(2, 4),
            dma(2, 4),
            dma(2),
            dma(2),
            dma(4),
            dma(4),
            dma(2, 2),
            dma(2, 2),
            dma(8, 4),
            dma(4, 4),
            dma(4, 4),
            dma(8, 4),
            dma(4, 4, 2),
            dma(4),
            dma(4),
            dma(2),
            dma(2),
            dma(2, 4),
            dma(2, 4),
            dma(4),
            dma(4),
            pltpu.SemaphoreType.DMA,
            pltpu.SemaphoreType.DMA,
        ],
        compiler_params=pltpu.CompilerParams(
            collective_id=0, has_side_effects=True, vmem_limit_bytes=62 * 2**20
        ),
    )(designs, prototypes, candidates, positives.reshape(1, ROWS))
    losses, design_grad, proto_grad = pl.pallas_call(
        settle,
        out_shape=(
            jax.ShapeDtypeStruct((1, ROWS), F32),
            jax.ShapeDtypeStruct((ROWS, D), BF16),
            jax.ShapeDtypeStruct((PAIR, D), F32),
        ),
        in_specs=[pl.BlockSpec(memory_space=pl.ANY)] * 3,
        out_specs=(pl.BlockSpec(memory_space=pl.ANY),) * 3,
        scratch_shapes=[vmem((1, ROWS), F32), vmem((ROWS, D), BF16), vmem((PAIR, D), F32), dma(2, 7)],
    )(losses, design_grad, proto_grad)
    return losses.reshape(ROWS), design_grad, proto_grad


def solution(mesh):
    return jax.shard_map(
        body,
        mesh=mesh,
        in_specs=(
            P(("proto", "design"), None),
            P("proto", None),
            P(("proto", "design"), None),
            P(("proto", "design")),
        ),
        out_specs=(
            P(("proto", "design")),
            P(("proto", "design"), None),
            P(("proto", "design"), None),
        ),
        check_vma=False,
    )
```

```python
import jax
import jax.numpy as jnp
from jax import lax
from jax.experimental import pallas as pl
from jax.experimental.pallas import tpu as pltpu
from jax.sharding import PartitionSpec as P

D = 1024
HALF = 512
TILE = 128
ROWS = 1024
SIDE = 4
BLOCKS = 16
CANDS = 24
PAIR = 2 * TILE
COLS = 256
LOW = -3.0e38
MESH = pl.DeviceIdType.MESH
BF16 = jnp.bfloat16
F32 = jnp.float32
I32 = jnp.int32


def remote(src, dst, send_sem, recv_sem, device):
    return pltpu.make_async_remote_copy(
        src_ref=src, dst_ref=dst, send_sem=send_sem, recv_sem=recv_sem, device_id=device, device_id_type=MESH
    )


def iota(shape, dim):
    return lax.broadcasted_iota(I32, shape, dim)


def to_column(row):
    n = row.shape[1]
    return jnp.sum(jnp.where(iota((n, n), 0) == iota((n, n), 1), jnp.broadcast_to(row, (n, n)), 0), axis=1, keepdims=True)


def to_row(col):
    n = col.shape[0]
    return jnp.sum(jnp.where(iota((n, n), 0) == iota((n, n), 1), jnp.broadcast_to(col, (n, n)), 0), axis=0, keepdims=True)


def gray(k):
    return k + (k // 2) * (1 - 2 * (k % 2))


def pair_of(n):
    s = jnp.where(n >= 1, 1, 0) + jnp.where(n >= 4, 1, 0) + jnp.where(n >= 9, 1, 0)
    m = n - s * s
    odd = m % 2
    return gray(s + odd * (m // 2 - s)), gray(m // 2 + odd * (s - m // 2))


def kernel(
    des, proto, cand, pos, loss_o, dg_o, pg_o,
    tab0, tab1, tab2, tab3, rr0, rr1, rr2, rr3,
    send, arr_m, arr_o, des_m, des_o, dt_m, dt_o, grads, stage, merge, from_up, from_down, from_y, far_y, runs, core_in, dg_s,
    prow, m_run, s_run, pick, total, req_v, req_in, order_v, req_own, req_s, order_s,
    ld_sem, des_sem, out_sem, loc_sem, own_sem, rq_s, rq_r, ag_s, ag_r, rl_s, rl_r, gy_s, gy_r, ha_s, ha_r, f_s, fm_r, fo_r, b_s, b_r,
    fy_s, fy_r, mg_s, mg_r, rs_s, rs_r, y_s, y_r, c_s, c_r,
):
    p, d = lax.axis_index("proto"), lax.axis_index("design")
    x, z, y, r = p // SIDE, p % SIDE, d // 2, d % 2
    tab, rr = (tab0, tab1, tab2, tab3), (rr0, rr1, rr2, rr3)

    def owner(ku, kv):
        return ((x + ku * (1 - r) + kv * r) % SIDE) * SIDE + (z + ku * r + kv * (1 - r)) % SIDE

    def along_u(k, core):
        return (owner(k, 0), y * 2 + core)

    def along_v(k, core):
        return (owner(0, k), y * 2 + core)

    def along_y(k):
        return (p, ((y + k) % SIDE) * 2 + r)

    def group(k):
        return pl.ds(((y + k) % SIDE) * 4, 4)

    sibling = (p, y * 2 + 1 - r)
    my_cols = pl.ds(pl.multiple_of(r * HALF, HALF), HALF)
    other_cols = pl.ds(pl.multiple_of((1 - r) * HALF, HALF), HALF)

    turns = (0, 1, 3, 2)

    def load(j):
        rows = pl.ds(pl.multiple_of(((y + turns[j]) % SIDE) * HALF, HALF), HALF)
        return pltpu.make_async_copy(proto.at[rows, my_cols], stage.at[j % 2], ld_sem.at[j])

    load(0).start()
    load(1).start()
    designs_in = [
        pltpu.make_async_copy(des.at[:, my_cols], des_m, des_sem.at[0]),
        pltpu.make_async_copy(des.at[:, other_cols], des_o, des_sem.at[1]),
    ]
    for c in designs_in:
        c.start()

    barrier = pltpu.get_barrier_semaphore()
    partners = [sibling]
    for k in (1, 2, 3):
        partners += [along_v(k, r), along_v(k, 1 - r), along_u(k, 1 - r), along_y(k)]
    partners += [along_u(1, r), along_u(3, r)]
    for q in partners:
        pl.semaphore_signal(barrier, inc=1, device_id=q, device_id_type=MESH)

    row = cand[...]
    col = to_column(row)
    same = (row >> 4) == (col >> 4)
    rank = jnp.sum(jnp.where(same & (iota((CANDS, CANDS), 1) < iota((CANDS, CANDS), 0)), 1, 0), axis=1, keepdims=True)
    slot = (col >> 4) * 2 + rank
    hit = slot == iota((CANDS, TILE), 1)
    wanted = jnp.sum(jnp.where(hit, (col & 15) + 1, 0), axis=0, keepdims=True) - 1
    req_v[...] = jnp.broadcast_to(wanted, (8, TILE))
    block = pos[...] >> 7
    spot = jnp.sum(jnp.where(col == block, slot, 0), axis=0, keepdims=True)
    prow[...] = spot * TILE + (pos[...] & 127)
    pltpu.make_async_copy(req_v, req_own, own_sem).start()

    pl.semaphore_wait(barrier, len(partners))

    req_in[0] = req_v[...]
    requests = [remote(req_v, req_in.at[1], rq_s.at[0], rq_r.at[1], sibling)]
    for k in (1, 2, 3):
        back = (SIDE - k) * 2
        requests.append(remote(req_v, req_in.at[back], rq_s.at[2 * k - 1], rq_r.at[back], along_v(k, r)))
        requests.append(remote(req_v, req_in.at[back + 1], rq_s.at[2 * k], rq_r.at[back + 1], along_u(k, 1 - r)))
    for c in requests:
        c.start()

    def own_chunk(k, way):
        low, count = ((0, 4), (2, 2), (0, 4), (0, 2))[k]
        part = pl.ds(((y + k) % SIDE) * 4 + low, count)
        dst = tab3 if way == 0 else tab1
        return remote(tab0.at[part], dst.at[part], ag_s.at[way, k], ag_r.at[way, k], along_u(1 if way == 0 else 3, r))

    for j in range(4):
        load(j).wait()
        for b in range(4):
            tab0[((y + turns[j]) % SIDE) * 4 + b] = stage[j % 2, TILE * b : TILE * (b + 1)].astype(BF16)
        if j < 2:
            own_chunk(turns[j], 0).start()
            own_chunk(turns[j], 1).start()
            load(j + 2).start()

    for c in designs_in:
        c.wait()

    @pl.loop(0, 4)
    def _(i):
        part = pl.ds(pl.multiple_of(i * COLS, COLS), COLS)
        dt_m[:, part] = des_m[part, :].T
        dt_o[:, part] = des_o[part, :].T

    for n in range(1, 8):
        remote(req_v, req_in.at[n], rq_s.at[0], rq_r.at[n], sibling).wait_recv()
    to_scalars = pltpu.make_async_copy(req_in, req_s, loc_sem.at[0])
    to_scalars.start()
    to_scalars.wait()

    def wanted_blocks(ku):
        first = owner(ku, 0) * 2
        for n in (0, 2, 3, 6, 7, 1, 4, 5):
            for i in range(2):
                val = tab[ku][jnp.maximum(req_s[n, 0, first + i], 0)]
                if n == 0:
                    arr_m[0, ku, i] = val
                else:
                    send[n, ku, i] = val
            if n not in (0, 4, 5):
                fetched(n, ku).start()

    def opposite(ku):
        for n in (4, 5):
            fetched(n, ku).start()

    def fetched(n, ku):
        k, so = n // 2, n % 2
        back = (SIDE - k) % SIDE
        if so == 0:
            return remote(send.at[n, ku], arr_m.at[back, ku], f_s.at[n, ku], fm_r.at[back, ku], along_v(k, r))
        return remote(send.at[n, ku], arr_o.at[back, ku], f_s.at[n, ku], fo_r.at[back, ku], along_v(k, 1 - r))

    def relay(way):
        part = pl.ds(4 * y + 2 * way, 2)
        src, to = (tab3, 1) if way == 0 else (tab1, 3)
        return remote(src.at[part], tab2.at[part], rl_s.at[way], rl_r.at[way], along_u(to, r))

    def share(k):
        return remote(tab2.at[group(0)], tab2.at[group(0)], gy_s.at[k], gy_r.at[SIDE - k], along_y(k))

    def hand(way, k):
        part = pl.ds(4 * y + (2 if k == 1 else 0), 2)
        src = tab3 if way == 0 else tab1
        return remote(src.at[part], src.at[part], ha_s.at[way, k // 2], ha_r.at[way, k // 2], along_y(k))

    for way in (0, 1):
        own_chunk(0, way).wait_recv()
        relay(way).start()
        hand(way, 1).start()
        hand(way, 3).start()
    for k in (3, 2):
        own_chunk(k, 0).start()
        own_chunk(k, 1).start()
    wanted_blocks(0)
    for way in (0, 1):
        relay(way).wait_recv()
    for k in (1, 3, 2):
        share(k).start()
    for way, ku in ((1, 1), (0, 3)):
        for k in (1, 2, 3):
            own_chunk(k, way).wait_recv()
        hand(way, 1).wait_recv()
        hand(way, 3).wait_recv()
        wanted_blocks(ku)
        opposite(0 if ku == 1 else 1)
    for k in (1, 2, 3):
        remote(tab2.at[group(0)], tab2.at[group(0)], gy_s.at[k], gy_r.at[k], sibling).wait_recv()
    wanted_blocks(2)
    opposite(3)
    opposite(2)

    for ku in range(4):
        first = owner(ku, 0) * 2
        eye = iota((8, TILE), 1)
        reqs = req_in[:, 0, :]
        ids = [jnp.sum(jnp.where(eye == first + i, reqs, 0), axis=1, keepdims=True) for i in range(2)]
        ids = jnp.concatenate(ids, axis=0)
        place = iota((BLOCKS, 1), 0)
        entry = (place % 8) * 2 + place // 8
        key = ids * BLOCKS + entry
        rank = jnp.sum(jnp.where(to_row(key) < key, 1, 0), axis=1, keepdims=True)
        at = rank == iota((BLOCKS, TILE), 1)
        follows = jnp.sum(jnp.where((to_row(key) < key) & (to_row(ids) == ids), 1, 0), axis=1, keepdims=True)
        lane = iota((BLOCKS, TILE), 1)
        rows = [
            jnp.sum(jnp.where(at, entry, 0), axis=0, keepdims=True),
            jnp.sum(jnp.where(at & (follows == 0), 1, 0), axis=0, keepdims=True),
            jnp.maximum(jnp.sum(jnp.where(ids <= lane, 1, 0), axis=0, keepdims=True) - 1, 0),
            jnp.sum(jnp.where(ids == lane, 1, 0), axis=0, keepdims=True),
        ]
        for i in range(4):
            order_v[ku, i : i + 1, :] = rows[i]
    order_copy = pltpu.make_async_copy(order_v, order_s, loc_sem.at[1])
    order_copy.start()
    pltpu.make_async_copy(req_v, req_own, own_sem).wait()

    def logits_of(ku, kv, part):
        o = owner(ku, kv)
        left = jnp.dot(arr_m[kv, ku].reshape(PAIR, HALF), dt_m[:, part], preferred_element_type=F32)
        right = jnp.dot(arr_o[ku, kv].reshape(PAIR, HALF), dt_o[:, part], preferred_element_type=F32)
        rows = iota((PAIR, COLS), 0)
        held = jnp.where(rows < TILE, req_own[0, o * 2], req_own[0, o * 2 + 1]) >= 0
        target = rows + o * PAIR == prow[:, part]
        return jnp.where(held, (left + right) * D**-0.5, LOW), target

    m_run[...] = jnp.full((1, ROWS), LOW, F32)
    s_run[...] = jnp.zeros((1, ROWS), F32)
    pick[...] = jnp.zeros((1, ROWS), F32)

    @pl.loop(0, 16)
    def _(n):
        ku, kv = pair_of(n)

        @pl.when(kv != 0)
        def _():
            remote(send.at[1, 0], arr_m.at[kv, ku], f_s.at[1, 0], fm_r.at[kv, ku], sibling).wait_recv()

        remote(send.at[1, 0], arr_o.at[ku, kv], f_s.at[1, 0], fo_r.at[ku, kv], sibling).wait_recv()

        @pl.loop(0, ROWS // COLS)
        def _(i):
            part = pl.ds(pl.multiple_of(i * COLS, COLS), COLS)
            logits, target = logits_of(ku, kv, part)
            pick[:, part] += jnp.sum(jnp.where(target, logits, 0.0), axis=0, keepdims=True)
            before = m_run[:, part]
            now = jnp.maximum(before, jnp.max(logits, axis=0, keepdims=True))
            m_run[:, part] = now
            s_run[:, part] = s_run[:, part] * jnp.exp(before - now) + jnp.sum(jnp.exp(logits - now), axis=0, keepdims=True)

    total[...] = m_run[...] + jnp.log(s_run[...])
    loss_o[...] = total[...] - pick[...]

    for n in range(1, 8):
        for ku in range(4):
            fetched(n, ku).wait_send()
    for c in requests:
        c.wait_send()
    for k in range(4):
        own_chunk(k, 0).wait_send()
        own_chunk(k, 1).wait_send()
    for way in (0, 1):
        relay(way).wait_send()
        hand(way, 1).wait_send()
        hand(way, 3).wait_send()
    for k in (1, 2, 3):
        share(k).wait_send()

    def back_mine(ku, kv, k):
        back = (SIDE - kv) % SIDE
        return remote(send.at[kv * 2, ku], rr[k].at[pl.ds(back * 4, 2)], b_s.at[kv * 2, ku], b_r.at[k, back, 0], along_v(kv, r))

    def back_other(ku, kv, k):
        back = (SIDE - ku) % SIDE
        return remote(send.at[ku * 2 + 1, kv], rr[k].at[pl.ds(back * 4 + 2, 2)], b_s.at[ku * 2 + 1, kv], b_r.at[k, back, 1], along_u(ku, 1 - r))

    def second_pass(n):
        ku, kv = pair_of(15 - n)

        @pl.loop(0, ROWS // COLS)
        def _(i):
            part = pl.ds(pl.multiple_of(i * COLS, COLS), COLS)
            logits, target = logits_of(ku, kv, part)
            grads[kv, ku, :, part] = (jnp.exp(logits - total[:, part]) - jnp.where(target, 1.0, 0.0)).astype(BF16)

        mine = jnp.dot(grads[kv, ku], des_m[...], preferred_element_type=F32).astype(BF16).reshape(2, TILE, HALF)
        send[kv * 2, ku] = mine

        @pl.when((ku == 0) & (kv == 0))
        def _():
            rr[0][0:2] = send[0, 0]

        for k in (1, 2, 3):

            @pl.when((ku == k) & (kv == 0))
            def _():
                rr[k][0:2] = send[0, k]

            @pl.when((ku == k) & (kv != 0))
            def _():
                back_mine(ku, kv, k).start()

        other = jnp.dot(grads[kv, ku], des_o[...], preferred_element_type=F32).astype(BF16).reshape(2, TILE, HALF)
        send[ku * 2 + 1, kv] = other
        for k in (1, 2, 3):

            @pl.when(kv == k)
            def _():
                back_other(ku, kv, k).start()

    def sums(ku):
        for n in range(1, 8):
            k, so = n // 2, n % 2
            remote(send.at[1, 0], rr[ku].at[pl.ds(2 * n, 2)], b_s.at[1, 0], b_r.at[ku, k, so], sibling).wait_recv()

        @pl.loop(0, TILE // 16)
        def _(i):
            part = pl.ds(pl.multiple_of(i * 16, 16), 16)
            acc = jnp.zeros((16, HALF), F32)
            for t in range(BLOCKS):
                val = rr[ku][order_s[ku, 0, t], part, :].astype(F32)
                acc = jnp.where(order_s[ku, 1, t] == 1, val, acc + val)
                runs[t] = acc
            for j in range(BLOCKS):
                val = runs[order_s[ku, 2, j]]
                tab[ku][j, part, :] = jnp.where(order_s[ku, 3, j] > 0, val, 0.0).astype(BF16)

    def design_grad(q, h):
        part = pl.ds(q * COLS, COLS)
        acc = stage.at[0, pl.ds(0, COLS)]
        acc[...] = jnp.zeros((COLS, HALF), F32)

        @pl.loop(0, 4)
        def _(k):
            lhs = grads[k, :, :, part] if h == 0 else grads[:, k, :, part]
            rhs = arr_m[k] if h == 0 else arr_o[k]
            acc[...] += lax.dot_general(
                lhs.reshape(ROWS, COLS), rhs.reshape(ROWS, HALF), (((0,), (0,)), ((), ())), preferred_element_type=F32
            )

        dg_s[q, h] = acc[...].astype(BF16)
        dg_out(q, h).start()

    def dg_out(q, h):
        cols = my_cols if h == 0 else other_cols
        return pltpu.make_async_copy(dg_s.at[q, h], dg_o.at[pl.ds(q * COLS, COLS), cols], out_sem.at[q, h])

    def far_along_y(k):
        return remote(tab2.at[group(k)], far_y.at[SIDE - k], fy_s.at[k], fy_r.at[SIDE - k], along_y(k))

    def far(way):
        part = pl.ds(4 * y + 2 * way, 2)
        return remote(tab2.at[part], merge.at[way], mg_s.at[way], mg_r.at[way], along_u(1 if way == 0 else 3, r))

    def near(k, way):
        if way == 0:
            return remote(tab1.at[group(k)], from_down.at[k], rs_s.at[0, k], rs_r.at[0, k], along_u(1, r))
        return remote(tab3.at[group(k)], from_up.at[k], rs_s.at[1, k], rs_r.at[1, k], along_u(3, r))

    def to_y(k):
        return remote(tab0.at[group(k)], from_y.at[SIDE - k], y_s.at[k], y_r.at[SIDE - k], along_y(k))

    pl.loop(0, 12)(second_pass)
    order_copy.wait()
    sums(2)
    for k in (1, 3, 2):
        far_along_y(k).start()
    pl.loop(12, 16)(second_pass)
    for kv in (1, 3, 2):
        back_mine(0, kv, 0).start()
    for ku in (0, 1, 3, 2):
        back_other(ku, 0, 0).start()
    design_grad(0, 0)
    sums(3)
    near(2, 1).start()
    sums(1)
    near(2, 0).start()
    for k in (1, 3):
        near(k, 1).start()
        near(k, 0).start()
    design_grad(0, 1)
    design_grad(1, 0)
    for k in (1, 3, 2):
        remote(tab2.at[group(0)], far_y.at[k], fy_s.at[k], fy_r.at[k], sibling).wait_recv()
    for b in range(4):
        val = tab2[4 * y + b].astype(F32)
        for k in (1, 2, 3):
            val += far_y[k, b].astype(F32)
        tab2[4 * y + b] = val.astype(BF16)
    far(0).start()
    far(1).start()
    design_grad(1, 1)
    sums(0)

    def add_near(k):
        near(k, 0).wait_recv()
        near(k, 1).wait_recv()
        for b in range(4):
            at = ((y + k) % SIDE) * 4 + b
            val = tab0[at].astype(F32) + from_up[k, b].astype(F32) + from_down[k, b].astype(F32)
            tab0[at] = val.astype(BF16)

    add_near(2)
    to_y(2).start()
    design_grad(2, 0)
    add_near(1)
    to_y(1).start()
    design_grad(2, 1)
    add_near(3)
    to_y(3).start()
    for way in (0, 1):
        src = tab1 if way == 0 else tab3
        far(way).wait_recv()
        for b in range(2):
            at = 4 * y + 2 * way + b
            src[at] = (src[at].astype(F32) + merge[way, b].astype(F32)).astype(BF16)
        near(0, way).start()
    design_grad(3, 0)
    design_grad(3, 1)
    add_near(0)
    for k in (1, 3, 2):
        remote(tab0.at[pl.ds(0, 4)], from_y.at[k], y_s.at[0], y_r.at[k], sibling).wait_recv()

    def reduced(b):
        val = tab0[4 * y + b].astype(F32)
        for k in (1, 2, 3):
            val += from_y[k, b].astype(F32)
        return val

    for i in range(2):
        stage[1, pl.ds(PAIR + i * TILE, TILE)] = reduced(2 * (1 - r) + i)
    cross = remote(stage.at[1, pl.ds(PAIR, PAIR)], core_in, c_s, c_r, sibling)
    cross.start()
    for i in range(2):
        stage[1, pl.ds(i * TILE, TILE)] = reduced(2 * r + i)
    outs = [pltpu.make_async_copy(stage.at[1, pl.ds(0, PAIR)], pg_o.at[:, my_cols], loc_sem.at[2])]
    outs[0].start()
    cross.wait_recv()
    outs.append(pltpu.make_async_copy(core_in, pg_o.at[:, other_cols], loc_sem.at[3]))
    outs[1].start()

    for kv in range(4):
        for ku in range(4):
            if kv:
                back_mine(ku, kv, ku).wait_send()
            back_other(ku, kv, kv).wait_send()
    for k in range(4):
        near(k, 0).wait_send()
        near(k, 1).wait_send()
        if k:
            far_along_y(k).wait_send()
            to_y(k).wait_send()
        for h in range(2):
            dg_out(k, h).wait()
    far(0).wait_send()
    far(1).wait_send()
    cross.wait_send()
    for c in outs:
        c.wait()


def settle(losses, design_grad, proto_grad, losses_o, design_grad_o, proto_grad_o, one, many, few, sems):
    moves = [(losses, one, losses_o)]
    for i in range(8):
        part = pl.ds(i * TILE, TILE)
        moves.append((design_grad.at[part], many.at[part], design_grad_o.at[part]))
    for i in range(4):
        part = pl.ds(i * 64, 64)
        moves.append((proto_grad.at[part], few.at[part], proto_grad_o.at[part]))
    reads = [pltpu.make_async_copy(a, b, sems.at[0, n]) for n, (a, b, c) in enumerate(moves)]
    writes = [pltpu.make_async_copy(b, c, sems.at[1, n]) for n, (a, b, c) in enumerate(moves)]
    for c in reads:
        c.start()
    for a, b in zip(reads, writes):
        a.wait()
        b.start()
    for c in writes:
        c.wait()


def body(designs, prototypes, candidates, positives):
    vmem = lambda shape, dtype: pltpu.VMEM(shape, dtype)
    dma = lambda *shape: pltpu.SemaphoreType.DMA(shape)
    blocks = (BLOCKS, TILE, HALF)
    pairs = (SIDE, SIDE, 2, TILE, HALF)
    losses, design_grad, proto_grad = pl.pallas_call(
        kernel,
        out_shape=(
            jax.ShapeDtypeStruct((1, ROWS), F32),
            jax.ShapeDtypeStruct((ROWS, D), BF16),
            jax.ShapeDtypeStruct((PAIR, D), F32),
        ),
        in_specs=[
            pl.BlockSpec(memory_space=pl.ANY),
            pl.BlockSpec(memory_space=pl.ANY),
            pl.BlockSpec(memory_space=pltpu.VMEM),
            pl.BlockSpec(memory_space=pltpu.VMEM),
        ],
        out_specs=(
            pl.BlockSpec(memory_space=pltpu.VMEM),
            pl.BlockSpec(memory_space=pl.ANY),
            pl.BlockSpec(memory_space=pl.ANY),
        ),
        scratch_shapes=[
            *[vmem(blocks, BF16) for _ in range(8)],
            vmem((8, SIDE, 2, TILE, HALF), BF16),
            vmem(pairs, BF16),
            vmem(pairs, BF16),
            vmem((ROWS, HALF), BF16),
            vmem((ROWS, HALF), BF16),
            vmem((HALF, ROWS), BF16),
            vmem((HALF, ROWS), BF16),
            vmem((SIDE, SIDE, PAIR, ROWS), BF16),
            vmem((2, HALF, HALF), F32),
            vmem((2, 2, TILE, HALF), BF16),
            vmem((4, 4, TILE, HALF), BF16),
            vmem((4, 4, TILE, HALF), BF16),
            vmem((4, 4, TILE, HALF), BF16),
            vmem((4, 4, TILE, HALF), BF16),
            vmem((BLOCKS, 16, HALF), F32),
            vmem((PAIR, HALF), F32),
            vmem((4, 2, COLS, HALF), BF16),
            vmem((1, ROWS), I32),
            *[vmem((1, ROWS), F32) for _ in range(4)],
            vmem((8, TILE), I32),
            vmem((8, 8, TILE), I32),
            vmem((4, 8, TILE), I32),
            pltpu.SMEM((8, TILE), I32),
            pltpu.SMEM((8, 8, TILE), I32),
            pltpu.SMEM((4, 8, TILE), I32),
            dma(4),
            dma(2),
            dma(4, 2),
            dma(4),
            pltpu.SemaphoreType.DMA,
            dma(8),
            dma(8),
            dma(2, 4),
            dma(2, 4),
            dma(2),
            dma(2),
            dma(4),
            dma(4),
            dma(2, 2),
            dma(2, 2),
            dma(8, 4),
            dma(4, 4),
            dma(4, 4),
            dma(8, 4),
            dma(4, 4, 2),
            dma(4),
            dma(4),
            dma(2),
            dma(2),
            dma(2, 4),
            dma(2, 4),
            dma(4),
            dma(4),
            pltpu.SemaphoreType.DMA,
            pltpu.SemaphoreType.DMA,
        ],
        compiler_params=pltpu.CompilerParams(
            collective_id=0, has_side_effects=True, vmem_limit_bytes=62 * 2**20
        ),
    )(designs, prototypes, candidates, positives.reshape(1, ROWS))
    losses, design_grad, proto_grad = pl.pallas_call(
        settle,
        out_shape=(
            jax.ShapeDtypeStruct((1, ROWS), F32),
            jax.ShapeDtypeStruct((ROWS, D), BF16),
            jax.ShapeDtypeStruct((PAIR, D), F32),
        ),
        in_specs=[pl.BlockSpec(memory_space=pl.ANY)] * 3,
        out_specs=(pl.BlockSpec(memory_space=pl.ANY),) * 3,
        scratch_shapes=[vmem((1, ROWS), F32), vmem((ROWS, D), BF16), vmem((PAIR, D), F32), dma(2, 13)],
    )(losses, design_grad, proto_grad)
    return losses.reshape(ROWS), design_grad, proto_grad


def solution(mesh):
    return jax.shard_map(
        body,
        mesh=mesh,
        in_specs=(
            P(("proto", "design"), None),
            P("proto", None),
            P(("proto", "design"), None),
            P(("proto", "design")),
        ),
        out_specs=(
            P(("proto", "design")),
            P(("proto", "design"), None),
            P(("proto", "design"), None),
        ),
        check_vma=False,
    )
```
